256 devices in a mesh: table: 32 (over x, z), rep: 8 (over y, core).
Axes of the slice: x: 4, y: 4, z: 8, core: 2. Of those that a mesh axis runs over, the one named last changes fastest.
Arguments:
- lengths: int32 [256, 2], P(('table', 'rep')), may hold values from 1 to 256, 320 in all within a row
- slots: int32 [512, 256], P(('table', 'rep')), may hold values from 0 to 1023, as said below
- requests: int32 [256, 32, 32], P(('table', 'rep')), may hold values from 0 to 2047, as said below
- counts: int32 [256, 32], P(('table', 'rep')), may hold values from 1 to 32, as said below
- codes: bfloat16 [65536, 256], P('table'), may hold values from -4 to 4
- scales: bfloat16 [65536, 8], P('table'), may hold values from 0.25 to 1
- accum: float32 [65536], P('table'), may hold values from 1 to 64
- conv_weight: bfloat16 [4, 3, 256, 256], replicated, may hold values from -0.21875 to 0.21875
- norm_gain: float32 [4, 256], replicated, may hold values from 0.5 to 1.5
- upstream: bfloat16 [512, 256, 256], P(('table', 'rep')), may hold values from -6 to 6
Outputs:
- new_rows: float32 [65536, 256], P('table')
- new_accum: float32 [65536], P('table')
- grad_conv: float32 [4, 3, 256, 256], replicated
- grad_gain: float32 [4, 256], replicated
The draws below stay inside these ranges and needn't reach their ends.
Inputs may be any that keep to these rules, and one draw needn't show every extreme that they name: requests[d, p, j] lies in [j * 64, (j + 1) * 64), so one device's requests to one owner are distinct; entries with j >= counts[d, p] are not in use. `counts`: one owner, the same for every device, gets 32 requests from each device. `slots`: every entry is p * 32 + j with j < counts[d, p] of the session's device d.
All inputs are finite; a program needn't handle non-finite values.
Results may differ from the reference program's by a relative error of at most 0.02.
Values may be sent and summed in bfloat16 or wider, within the bound.
No kernel may reach another device: no remote copies, remote signals or barrier semaphores. Data moves between devices by JAX's collectives and lax.ppermute only.
A program may use at most 64 MiB of HBM per device.

```python
import math
import jax
import jax.numpy as jnp
import numpy as np
from jax import lax

C = 256
GROUP = 32
LAYERS = 4
TAPS = 3
LEN = 256
SESS_DEV = 2
ROWS_DEV = 2048
CAP = 32
OWNERS = 32
SENDERS = 256
SESSIONS = 512
ROWS = 65536


def layout(key):
    keys = jax.random.split(key, 5)
    counts = jax.random.randint(keys[0], (SENDERS, OWNERS), 1, CAP + 1, dtype=jnp.int32)
    hottest = jax.random.randint(keys[1], (), 0, OWNERS, dtype=jnp.int32)
    counts = jnp.where(jnp.arange(OWNERS, dtype=jnp.int32)[None, :] == hottest, CAP, counts)
    stride = ROWS_DEV // CAP
    offsets = jax.random.randint(keys[2], (SENDERS, OWNERS, CAP), 0, stride, dtype=jnp.int32)
    requests = jnp.arange(CAP, dtype=jnp.int32)[None, None, :] * stride + offsets
    owner_pick = jax.random.randint(keys[3], (SESSIONS, LEN), 0, OWNERS, dtype=jnp.int32)
    entry_pick = jax.random.randint(keys[4], (SESSIONS, LEN), 0, CAP, dtype=jnp.int32)
    sender_of = jnp.arange(SESSIONS, dtype=jnp.int32) // SESS_DEV
    in_use = counts[sender_of[:, None], owner_pick]
    slots = owner_pick * CAP + entry_pick % in_use
    return (requests, counts, slots)


def draw_requests(key, part):
    requests, counts, slots = layout(key)
    return requests


def draw_counts(key, part):
    requests, counts, slots = layout(key)
    return counts


def draw_slots(key, part):
    requests, counts, slots = layout(key)
    return slots


def level_of(key, dims, cuts, low, top_value):
    level, own = 1.0, jax.random.fold_in(key, 6)
    for dim, shards_of in cuts:
        steps = jnp.exp(jax.random.uniform(jax.random.fold_in(own, dim), (shards_of,), jnp.float32, low / len(cuts), top_value / len(cuts)))
        level = level * jnp.repeat(steps, dims[dim] // shards_of).reshape([-1 if axis == dim else 1 for axis in range(len(dims))])
    return level


def profile(number_of, total, limit, skew):
    weights = [(1 << 20) // math.isqrt(grade ** skew) + 1 for grade in range(2, number_of + 1)]
    spare, holding = total - limit - (number_of - 1), [1] * (number_of - 1)
    while spare > 0:
        movable = [i for i in range(number_of - 1) if holding[i] < limit]
        whole, budget = sum([weights[i] for i in movable]), spare
        for i in movable:
            more = min(limit - holding[i], max(1, budget * weights[i] // whole), spare)
            holding[i] = holding[i] + more
            spare = spare - more
    return np.array([limit] + holding)


def ragged(own_key, number_of, total, limit, slope):
    if number_of == 2:
        one = jax.random.randint(own_key, (), max(1, total - limit), min(limit, total - 1) + 1)
        return jnp.stack([one, total - one])
    sizes = jnp.asarray(profile(number_of, total, limit, slope), jnp.int32)
    pairs = (number_of - 1) // 2
    source_of, receiver = sizes[1:1 + 2 * pairs:2], sizes[2:2 + 2 * pairs:2]
    margin = jnp.minimum(source_of - 1, limit - receiver)
    moved = jax.random.randint(jax.random.fold_in(own_key, 1), (pairs,), 0, 1 << 20) % (margin + 1)
    sizes = sizes.at[1:1 + 2 * pairs:2].set(source_of - moved).at[2:2 + 2 * pairs:2].set(receiver + moved)
    return sizes[jax.random.permutation(jax.random.fold_in(own_key, 2), number_of)]


def scatter_about(rng, shape, deviation, bound, cuts=(), kind=jnp.bfloat16):
    level = level_of(rng, shape, cuts, -0.22, 0.18) if cuts else 1.0
    drawn = jax.random.normal(rng, shape, jnp.float32) * deviation * level
    return jnp.minimum(jnp.maximum(drawn, -bound), bound).astype(kind)


def setup_inputs(seed: int = 0) -> dict:
    arg_keys = jax.random.split(jax.random.key(seed), 11)
    return {
        "lengths": jax.vmap(lambda own: ragged(own, SESS_DEV, SESS_DEV * LEN * 5 // 8, LEN, 2))(jax.random.split(arg_keys[0], SENDERS)).reshape((SENDERS, SESS_DEV)).astype(jnp.int32),
        "slots": draw_slots(jax.random.fold_in(arg_keys[10], 71), 0),
        "requests": draw_requests(jax.random.fold_in(arg_keys[10], 71), 0),
        "counts": draw_counts(jax.random.fold_in(arg_keys[10], 71), 0),
        "codes": scatter_about(arg_keys[4], (ROWS, C), 1.0, 4.0, ((0, 32),)),
        "scales": jnp.clip(jnp.exp(math.log(1.0) - 1.3862944 * jax.random.uniform(arg_keys[5], (ROWS, C // GROUP), jnp.float32) ** level_of(arg_keys[5], (ROWS, C // GROUP), ((0, 32),), -0.2, 0.2)), 0.25, 1.0).astype(jnp.bfloat16),
        "accum": jnp.clip(jnp.exp(math.log(64.0) - 4.158883 * jax.random.uniform(arg_keys[6], (ROWS,), jnp.float32) ** level_of(arg_keys[6], (ROWS,), ((0, 32),), -0.2, 0.2)), 1.0, 64.0),
        "conv_weight": scatter_about(arg_keys[7], (LAYERS, TAPS, C, C), (TAPS * C) ** -0.5, 0.21875),
        "norm_gain": jnp.clip(1.0 + 0.1 * jax.random.normal(arg_keys[8], (LAYERS, C), jnp.float32), 0.5, 1.5),
        "upstream": scatter_about(arg_keys[9], (SESSIONS, LEN, C), 1.0, 6.0, ((0, 256),)),
    }


DILATIONS = (1, 2, 4, 8)
LEARN_RATE = 0.5

def dequantize(row_codes, row_scales):
    count, channels = row_codes.shape
    groups = row_scales.shape[1]
    spread = row_codes.astype(jnp.float32).reshape(count, groups, channels // groups)
    return (spread * row_scales.astype(jnp.float32)[:, :, None]).reshape(count, channels)

def shift_time(values, offset):
    padded = jnp.pad(values, ((0, 0), (offset, 0), (0, 0)))
    return padded[:, :values.shape[1], :]

def dilated(values, kernel, spread):
    sessions, steps_len, channels = values.shape
    total = jnp.zeros((sessions * steps_len, kernel.shape[2]), jnp.float32)
    for tap in range(kernel.shape[0]):
        moved = shift_time(values, tap * spread).reshape(sessions * steps_len, channels)
        total = total + jnp.dot(moved, kernel[tap], preferred_element_type=jnp.float32)
    return total.reshape(sessions, steps_len, kernel.shape[2])

def normed(values, gain):
    center = values - lax.optimization_barrier(jnp.mean(values, axis=-1, keepdims=True))
    spread = lax.optimization_barrier(jnp.mean(center * center, axis=-1, keepdims=True))
    return center * lax.rsqrt(spread + 1e-05) * gain

def stack(inputs, kernels, gains):
    hidden = inputs
    for block_index in range(2):
        lower = 2 * block_index
        first = dilated(hidden, kernels[lower], DILATIONS[lower])
        first = jax.nn.silu(normed(first, gains[lower])).astype(jnp.bfloat16)
        second = dilated(first, kernels[lower + 1], DILATIONS[lower + 1])
        second = jax.nn.silu(normed(second, gains[lower + 1]))
        hidden = (second + hidden.astype(jnp.float32)).astype(jnp.bfloat16)
    return hidden

def embed(fetched, sess_slots, sess_lengths):
    gathered = fetched.astype(jnp.bfloat16)[sess_slots]
    inside = jnp.arange(sess_slots.shape[1], dtype=jnp.int32)[None, :] < sess_lengths[:, None]
    return (jnp.where(inside[:, :, None], gathered, jnp.zeros_like(gathered)), inside)

def slot_sums(input_grad, inside, sess_slots, slot_total):
    channels = input_grad.shape[2]
    masked = input_grad.astype(jnp.float32) * inside[:, :, None].astype(jnp.float32)
    return jax.ops.segment_sum(masked.reshape(-1, channels), sess_slots.reshape(-1), num_segments=slot_total)

def adagrad(rows_now, accum_now, gradient):
    accum_next = accum_now + lax.optimization_barrier(jnp.mean(gradient * gradient, axis=1))
    return (rows_now - LEARN_RATE * gradient * lax.rsqrt(accum_next)[:, None], accum_next)

def local_step(fetched, sess_slots, sess_lengths, conv_weight, norm_gain, sess_upstream, slot_total):
    inputs, inside = embed(fetched, sess_slots, sess_lengths)
    states, pullback = jax.vjp(stack, inputs, conv_weight, norm_gain)
    cotangent = jnp.where(inside[:, :, None], sess_upstream, jnp.zeros_like(sess_upstream))
    input_grad, weight_grad, gain_grad = pullback(cotangent)
    slot_grad = slot_sums(input_grad, inside, sess_slots, slot_total).astype(jnp.bfloat16)
    return (slot_grad, weight_grad.astype(jnp.float32), gain_grad)

def reference(lengths, slots, requests, counts, codes, scales, accum, conv_weight, norm_gain, upstream):
    owners = requests.shape[1]
    capacity = requests.shape[2]
    sess_count = lengths.shape[1]
    channels = codes.shape[1]
    row_owned = codes.shape[0] // owners

    def one_device(carry, index):
        table_grad, weight_total, gain_total = carry
        local_requests = lax.dynamic_index_in_dim(requests, index, 0, keepdims=False)
        local_counts = lax.dynamic_index_in_dim(counts, index, 0, keepdims=False)
        global_rows = (jnp.arange(owners, dtype=jnp.int32)[:, None] * row_owned + local_requests).reshape(-1)
        filled = (jnp.arange(capacity, dtype=jnp.int32)[None, :] < local_counts[:, None]).reshape(-1)
        row_codes = jnp.where(filled[:, None], codes[global_rows], jnp.zeros((), codes.dtype))
        row_scales = jnp.where(filled[:, None], scales[global_rows], jnp.zeros((), scales.dtype))
        fetched = dequantize(row_codes, row_scales)
        start = (index * sess_count).astype(jnp.int32)
        sess_slots = lax.dynamic_slice_in_dim(slots, start, sess_count, 0)
        sess_upstream = lax.dynamic_slice_in_dim(upstream, start, sess_count, 0)
        sess_lengths = lax.dynamic_index_in_dim(lengths, index, 0, keepdims=False)
        slot_grad, weight_grad, gain_grad = local_step(fetched, sess_slots, sess_lengths, conv_weight, norm_gain, sess_upstream, owners * capacity)
        weighted = slot_grad.astype(jnp.float32) * filled[:, None].astype(jnp.float32)
        table_grad = table_grad.at[global_rows].add(weighted)
        return ((table_grad, weight_total + weight_grad, gain_total + gain_grad), None)
    start_carry = (jnp.zeros((codes.shape[0], channels), jnp.float32), jnp.zeros(conv_weight.shape, jnp.float32), jnp.zeros(norm_gain.shape, jnp.float32))
    senders = jnp.arange(lengths.shape[0], dtype=jnp.int32)
    (table_grad, weight_total, gain_total), unused = lax.scan(one_device, start_carry, senders)
    new_rows, new_accum = adagrad(dequantize(codes, scales), accum, table_grad)
    return (new_rows, new_accum, weight_total, gain_total)
```

```python
import functools

import jax
import jax.numpy as jnp
from jax import lax
from jax.experimental import pallas as pl
from jax.experimental.pallas import tpu as pltpu
from jax.sharding import Mesh
from jax.sharding import PartitionSpec as P

DILATIONS = (1, 2, 4, 8)
LEARN_RATE = 0.5
BF = jnp.bfloat16
F32 = jnp.float32
LAYERS, TAPS, C = 4, 3, 256
GROUP = 32
LEN = 256
PACKED = 320
STEP = 64
PIECE = 96
TAIL = 8
SLAB = PIECE + TAIL
NT = (((1,), (1,)), ((), ()))
TN = (((0,), (0,)), ((), ()))
PARAMS = pltpu.CompilerParams(vmem_limit_bytes=40 * 1024 * 1024)
SMEM = pl.BlockSpec(memory_space=pltpu.SMEM)
VMEM = pl.BlockSpec(memory_space=pltpu.VMEM)


def call(kernel, outs, args, scalars=0, scratch=(), flops=0):
    specs = [SMEM] * scalars + [VMEM] * (len(args) - scalars)
    return pl.pallas_call(
        kernel,
        out_shape=outs,
        in_specs=specs,
        out_specs=jax.tree.map(lambda _: VMEM, outs),
        scratch_shapes=list(scratch),
        compiler_params=PARAMS,
        cost_estimate=pl.CostEstimate(flops=flops, bytes_accessed=1 << 20, transcendentals=0),
    )(*args)


def shape(dims, dtype):
    return jax.ShapeDtypeStruct(dims, dtype)


def iota(dims, axis):
    return lax.broadcasted_iota(jnp.int32, dims, axis)


def dequantize_kernel(codes_ref, scales_ref, wide_ref, narrow_ref):
    groups = scales_ref.shape[1]
    spread = (iota((groups, C), 1) // GROUP == iota((groups, C), 0)).astype(F32).astype(BF)
    rows = codes_ref.shape[0]
    for start in range(0, rows, 256):
        part = pl.ds(start, 256)
        scale = jnp.dot(scales_ref[part, :], spread, preferred_element_type=F32)
        wide = codes_ref[part, :].astype(F32) * scale
        wide_ref[part, :] = wide
        narrow_ref[part, :] = wide.astype(BF)


def fetch_kernel(asked_ref, table_ref, out_ref):
    senders, cap = asked_ref.shape
    rows = table_ref.shape[0]
    stride = rows // cap
    asked = asked_ref[...].astype(F32).astype(BF)
    part = 256
    for start in range(0, senders * cap, part):
        line = iota((part, senders), 0) + start
        pick = (line // cap == iota((part, senders), 1)).astype(F32).astype(BF)
        lists = jnp.dot(pick, asked, preferred_element_type=F32)
        entry = (iota((part, cap), 0) + start) % cap
        own = jnp.where(entry == iota((part, cap), 1), lists, 0.0)
        offset = jnp.sum(own, axis=1, keepdims=True).astype(jnp.int32)
        entry = (iota((part, 1), 0) + start) % cap
        target = jnp.where(offset >= 0, entry * stride + offset, -1)
        chosen = (iota((part, rows), 1) == target).astype(F32).astype(BF)
        got = jnp.dot(chosen, table_ref[...], preferred_element_type=F32)
        out_ref[pl.ds(start, part), :] = got.astype(BF)


def sigmoid(values):
    return 0.5 + 0.5 * jnp.tanh(0.5 * values)


def train_kernel(
    place_ref,
    slot_col_ref,
    slot_row_ref,
    fetched_ref,
    weight_ref,
    gain_ref,
    upstream_ref,
    slot_grad_ref,
    keep_ref,
    send_ref,
    held_ref,
    conv_ref,
    unit_ref,
    scale_ref,
    grad_ref,
    wide_ref,
    weight_grad_ref,
):
    split, x, y, core = place_ref[0], place_ref[1], place_ref[2], place_ref[3]
    steps = range(0, PACKED, STEP)
    line = iota((PACKED, C), 0)
    since = jnp.where(line >= split, line - split, line)
    until = jnp.where(line >= split, PACKED - line, split - line)

    slots = fetched_ref.shape[0]
    chosen = (iota((PACKED, slots), 1) == slot_col_ref[...]).astype(F32).astype(BF)
    first = jnp.dot(chosen, fetched_ref[...], preferred_element_type=F32)
    held_ref[0] = first.astype(BF)

    for layer in range(LAYERS):
        gap = DILATIONS[layer]
        now = held_ref[layer].astype(F32)
        taps = [held_ref[layer]]
        for tap in (1, 2):
            moved = pltpu.roll(now, tap * gap, 0)
            taps.append(jnp.where(since >= tap * gap, moved, 0.0).astype(BF))
        base = layer * TAPS * C
        conv_ref[...] = jnp.dot(
            jnp.concatenate(taps, axis=1),
            weight_ref[pl.ds(base, TAPS * C), :],
            preferred_element_type=F32,
        )
        gain = gain_ref[pl.ds(layer, 1), :]
        for start in steps:
            part = pl.ds(start, STEP)
            value = conv_ref[part, :]
            center = value - jnp.mean(value, axis=1, keepdims=True)
            spread = jnp.mean(center * center, axis=1, keepdims=True)
            scale = lax.rsqrt(spread + 1e-5)
            unit = center * scale
            unit_ref[layer, part, :] = unit
            scale_ref[layer, part, :] = jnp.broadcast_to(scale, (STEP, 128))
            if layer + 1 < LAYERS:
                gained = unit * gain
                after = gained * sigmoid(gained)
                if layer % 2 == 1:
                    after = after + held_ref[layer - 1, part, :].astype(F32)
                held_ref[layer + 1, part, :] = after.astype(BF)

    source = iota((PACKED, 1), 0)
    source = jnp.where(source >= split, source + (LEN - split), source)
    packer = (iota((PACKED, 2 * LEN), 1) == source).astype(F32).astype(BF)
    grad_ref[...] = jnp.dot(packer, upstream_ref[...], preferred_element_type=F32)

    gain_rows = [None] * LAYERS
    for layer in reversed(range(LAYERS)):
        gap = DILATIONS[layer]
        gain = gain_ref[pl.ds(layer, 1), :]
        total = jnp.zeros((8, C), F32)
        for start in steps:
            part = pl.ds(start, STEP)
            unit = unit_ref[layer, part, :]
            scale = scale_ref[layer, part, :]
            gained = unit * gain
            gate = sigmoid(gained)
            inner = grad_ref[part, :] * (gate * (1.0 + gained * (1.0 - gate)))
            total = total + jnp.sum((inner * unit).reshape(STEP // 8, 8, C), axis=0)
            inner = inner * gain
            mean = jnp.mean(inner, axis=1, keepdims=True)
            slope = jnp.mean(inner * unit, axis=1, keepdims=True)
            outer = inner - mean - unit * slope
            conv_ref[part, :] = outer * jnp.concatenate([scale, scale], axis=1)
        gain_rows[layer] = jnp.sum(total, axis=0, keepdims=True)
        now = conv_ref[...]
        wide_ref[:, 0:C] = now.astype(BF)
        for tap in (1, 2):
            moved = pltpu.roll(now, PACKED - tap * gap, 0)
            moved = jnp.where(until > tap * gap, moved, 0.0)
            wide_ref[:, tap * C : (tap + 1) * C] = moved.astype(BF)

        below = jnp.zeros((PACKED, C), F32)
        for tap in range(TAPS):
            kernel = weight_ref[pl.ds((layer * TAPS + tap) * C, C), :]
            below = below + lax.dot_general(
                wide_ref[:, tap * C : (tap + 1) * C], kernel, NT, preferred_element_type=F32
            )
        if layer % 2 == 0:
            if layer == 2:
                skip = jnp.dot(packer, upstream_ref[...], preferred_element_type=F32)
            else:
                skip = held_ref[4].astype(F32)
            below = below + skip
        rounded = below.astype(BF)
        grad_ref[...] = rounded.astype(F32)
        if layer == 2:
            held_ref[4] = rounded

        weight_grad = lax.dot_general(
            held_ref[layer], wide_ref[...], TN, preferred_element_type=F32
        )
        for tap in range(TAPS):
            weight_grad_ref[pl.ds(tap * C, C), :] = weight_grad[:, tap * C : (tap + 1) * C]

        for pair in range(4):
            even = weight_grad_ref[pl.ds(2 * pair * PIECE, PIECE), :]
            odd = weight_grad_ref[pl.ds((2 * pair + 1) * PIECE, PIECE), :]
            tail = jnp.zeros((TAIL, C), F32)
            even_tail = tail
            if layer == 0 and pair == 0:
                exact = jnp.concatenate(gain_rows + gain_rows, axis=0)
                high = exact.astype(BF).astype(F32)
                even_tail = jnp.where(iota((TAIL, C), 0) < LAYERS, high, exact - high)
            even = jnp.concatenate([even, even_tail], axis=0)
            odd = jnp.concatenate([odd, tail], axis=0)
            place = ((layer - x + 4) % 4) * 4 + (pair - y + 4) % 4
            keep_ref[place] = jnp.where(core == 0, even, odd).astype(BF)
            send_ref[place] = jnp.where(core == 0, odd, even).astype(BF)

    mine = grad_ref[...].astype(BF)
    for start in range(0, slots, 256):
        here = iota((256, PACKED), 0) + start == slot_row_ref[...]
        here = here.astype(F32).astype(BF)
        summed = jnp.dot(here, mine, preferred_element_type=F32)
        slot_grad_ref[pl.ds(start, 256), :] = summed.astype(BF)


def settle(total):
    tail = total[PIECE:SLAB, :]
    exact = tail + pltpu.roll(tail, LAYERS, 0)
    high = exact.astype(BF).astype(F32)
    tail = jnp.where(iota((TAIL, C), 0) < LAYERS, high, exact - high)
    return jnp.concatenate([total[:PIECE, :], tail], axis=0).astype(BF)


def core_sum_kernel(keep_ref, got_ref, *out_refs):
    for at in range(16):
        total = keep_ref[at].astype(F32) + got_ref[at].astype(F32)
        out_refs[at // 4][at % 4] = settle(total)


def four_sum_kernel(a_ref, b_ref, c_ref, d_ref, *out_refs):
    for at in range(a_ref.shape[0]):
        left = a_ref[at].astype(F32) + b_ref[at].astype(F32)
        right = c_ref[at].astype(F32) + d_ref[at].astype(F32)
        out_refs[at][0] = settle(left + right)


def two_sum_kernel(a_ref, b_ref, out_ref):
    out_ref[0] = settle(a_ref[0].astype(F32) + b_ref[0].astype(F32))


def spread_kernel(place_ref, *refs):
    blocks, conv_ref, gain_ref = refs[:8], refs[8], refs[9]
    x, y, core = place_ref[1], place_ref[2], place_ref[3]
    for at in range(8):
        layer = (x + at % 4) % 4
        side = core if at < 4 else 1 - core
        for inner in range(4):
            number = layer * 8 + ((y + inner) % 4) * 2 + side
            block = blocks[at][inner].astype(F32)
            conv_ref[pl.ds(pl.multiple_of(number * PIECE, PIECE), PIECE), :] = block[:PIECE, :]

            @pl.when(number == 0)
            def _():
                tail = block[PIECE:, :]
                gain_ref[...] = (tail + pltpu.roll(tail, LAYERS, 0))[:LAYERS, :]


def scatter_kernel(place_ref, asked_ref, got_ref, keep_ref, send_ref):
    y, core = place_ref[2], place_ref[3]
    lines = asked_ref.shape[1]
    for pair in range(4):
        parts = []
        for side in range(2):
            row = iota((256, lines), 0) + (2 * pair + side) * 256
            here = (row == asked_ref[...]).astype(F32).astype(BF)
            parts.append(jnp.dot(here, got_ref[...], preferred_element_type=F32))
        even, odd = parts
        place = (pair - y + 4) % 4
        keep_ref[place] = jnp.where(core == 0, even, odd).astype(BF)
        send_ref[place] = jnp.where(core == 0, odd, even).astype(BF)


def row_core_sum_kernel(keep_ref, got_ref, *out_refs):
    for at in range(4):
        out_refs[at][...] = (keep_ref[at].astype(F32) + got_ref[at].astype(F32)).astype(BF)


def row_four_sum_kernel(a_ref, b_ref, c_ref, d_ref, out_ref):
    left = a_ref[...].astype(F32) + b_ref[...].astype(F32)
    right = c_ref[...].astype(F32) + d_ref[...].astype(F32)
    out_ref[...] = (left + right).astype(BF)


def adagrad_kernel(place_ref, *refs):
    blocks, table_ref, accum_ref, rows_ref, next_ref = refs[:8], *refs[8:]
    y, core = place_ref[2], place_ref[3]
    for at in range(8):
        side = core if at < 4 else 1 - core
        number = ((y + at % 4) % 4) * 2 + side
        part = pl.ds(pl.multiple_of(number * 256, 256), 256)
        gradient = blocks[at][...].astype(F32)
        grown = accum_ref[part, :] + jnp.mean(gradient * gradient, axis=1, keepdims=True)
        next_ref[part, :] = grown
        rows_ref[part, :] = table_ref[part, :] - LEARN_RATE * gradient * lax.rsqrt(grown)


def shifted(values, axis, size, offset):
    return lax.ppermute(values, axis, [(i, (i + offset) % size) for i in range(size)])


def crossed(values, axis, size, bits):
    return lax.ppermute(values, axis, [(i, i ^ bits) for i in range(size)])


def body(lengths, slots, requests, counts, codes, scales, accum, conv_weight, norm_gain, upstream):
    table_axes = ("x", "z")
    owners = requests.shape[1]
    cap = requests.shape[2]
    rows = codes.shape[0]
    stride = rows // cap
    split = lengths[0, 0]
    place = jnp.stack(
        [split, lax.axis_index("x"), lax.axis_index("y"), lax.axis_index("core")]
    ).astype(jnp.int32)

    entry = jnp.arange(cap, dtype=jnp.int32)[None, :]
    wanted = jnp.where(entry < counts[0][:, None], requests[0] - entry * stride, -1)
    asked = lax.all_to_all(wanted, table_axes, split_axis=0, concat_axis=0, tiled=True)

    wide, narrow = call(
        dequantize_kernel,
        [shape((rows, C), F32), shape((rows, C), BF)],
        [codes, scales],
        flops=1 << 24,
    )
    order = jnp.arange(PACKED, dtype=jnp.int32)
    order = order + jnp.where(order >= split, LEN - split, 0)
    match = order[:, None] == jnp.arange(2 * LEN, dtype=jnp.int32)[None, :]
    packed = jnp.sum(jnp.where(match, slots.reshape(1, 2 * LEN), 0), axis=1)

    sending = call(fetch_kernel, shape((owners * cap, C), BF), [asked, narrow], flops=1 << 30)
    fetched = lax.all_to_all(
        sending.reshape(owners, cap, C), table_axes, split_axis=0, concat_axis=0, tiled=True
    ).reshape(owners * cap, C)

    slab16 = shape((16, SLAB, C), BF)
    slot_grad, keep, send = call(
        train_kernel,
        [shape((owners * cap, C), BF), slab16, slab16],
        [
            place,
            packed.reshape(PACKED, 1),
            packed.reshape(1, PACKED),
            fetched,
            conv_weight.reshape(LAYERS * TAPS * C, C),
            norm_gain,
            upstream.reshape(2 * LEN, C),
        ],
        scalars=1,
        scratch=[
            pltpu.VMEM((LAYERS + 1, PACKED, C), BF),
            pltpu.VMEM((PACKED, C), F32),
            pltpu.VMEM((LAYERS, PACKED, C), F32),
            pltpu.VMEM((LAYERS, PACKED, 128), F32),
            pltpu.VMEM((PACKED, C), F32),
            pltpu.VMEM((PACKED, TAPS * C), BF),
            pltpu.VMEM((TAPS * C, C), F32),
        ],
        flops=1 << 32,
    )

    got = crossed(send, "core", 2, 1)
    returned = lax.all_to_all(
        slot_grad.reshape(owners, cap, C), table_axes, split_axis=0, concat_axis=0, tiled=True
    ).reshape(owners * cap, C)

    slab4, slab1 = shape((4, SLAB, C), BF), shape((1, SLAB, C), BF)
    parts = call(core_sum_kernel, [slab4] * 4, [keep, got])
    parts = [parts[0]] + [shifted(parts[k], "x", 4, k) for k in (1, 2, 3)]
    parts = call(four_sum_kernel, [slab1] * 4, parts)
    parts = [parts[0]] + [shifted(parts[k], "y", 4, k) for k in (1, 2, 3)]
    (part,) = call(four_sum_kernel, [slab1], parts)
    (part,) = call(
        four_sum_kernel, [slab1], [part] + [crossed(part, "z", 8, k) for k in (1, 2, 3)]
    )
    part = call(two_sum_kernel, slab1, [part, crossed(part, "z", 8, 4)])
    parts = jnp.concatenate([part] + [shifted(part, "y", 4, -k) for k in (1, 2, 3)], axis=0)
    parts = [parts] + [shifted(parts, "x", 4, -k) for k in (1, 2, 3)]
    parts = parts + [crossed(part, "core", 2, 1) for part in parts]
    grad_conv, grad_gain = call(
        spread_kernel,
        [shape((LAYERS * TAPS * C, C), F32), shape((LAYERS, C), F32)],
        [place] + parts,
        scalars=1,
    )

    target = jnp.where(asked >= 0, asked + entry * stride, -1).reshape(1, owners * cap)
    block4, block1 = shape((4, 256, C), BF), shape((256, C), BF)
    keep_rows, send_rows = call(
        scatter_kernel, [block4, block4], [place, target, returned], scalars=1, flops=1 << 30
    )
    got_rows = crossed(send_rows, "core", 2, 1)
    sums = call(row_core_sum_kernel, [block1] * 4, [keep_rows, got_rows])
    sums = [sums[0]] + [shifted(sums[k], "y", 4, k) for k in (1, 2, 3)]
    mine = call(row_four_sum_kernel, block1, sums)
    blocks = [mine] + [shifted(mine, "y", 4, -k) for k in (1, 2, 3)]
    blocks = blocks + [crossed(block, "core", 2, 1) for block in blocks]
    new_rows, new_accum = call(
        adagrad_kernel,
        [shape((rows, C), F32), shape((rows, 1), F32)],
        [place] + blocks + [wide, accum.reshape(rows, 1)],
        scalars=1,
    )
    return (
        new_rows,
        new_accum.reshape(rows),
        grad_conv.reshape(conv_weight.shape),
        grad_gain,
    )


def solution(mesh):
    fine = Mesh(mesh.devices.reshape(4, 8, 4, 2), ("x", "z", "y", "core"))
    every = ("x", "z", "y", "core")
    table = ("x", "z")
    return jax.shard_map(
        body,
        mesh=fine,
        in_specs=(
            P(every, None),
            P(every, None),
            P(every, None, None),
            P(every, None),
            P(table, None),
            P(table, None),
            P(table),
            P(),
            P(),
            P(every, None, None),
        ),
        out_specs=(P(table, None), P(table), P(), P()),
        check_vma=False,
    )
```

```python
import functools

import jax
import jax.numpy as jnp
from jax import lax
from jax.experimental import pallas as pl
from jax.experimental.pallas import tpu as pltpu
from jax.sharding import Mesh
from jax.sharding import PartitionSpec as P

DILATIONS = (1, 2, 4, 8)
LEARN_RATE = 0.5
BF = jnp.bfloat16
F32 = jnp.float32
LAYERS, TAPS, C = 4, 3, 256
GROUP = 32
LEN = 256
PACKED = 320
STEP = 64
PIECE = 96
TAIL = 8
SLAB = PIECE + TAIL
NT = (((1,), (1,)), ((), ()))
TN = (((0,), (0,)), ((), ()))
SMEM = pl.BlockSpec(memory_space=pltpu.SMEM)
VMEM = pl.BlockSpec(memory_space=pltpu.VMEM)
ANY = pl.BlockSpec(memory_space=pl.ANY)
HBM = pl.BlockSpec(memory_space=pltpu.HBM)


def call(kernel, outs, args, specs=None, out_specs=None, scratch=(), flops=0, limit=8):
    if specs is None:
        specs = [VMEM] * len(args)
    if out_specs is None:
        out_specs = jax.tree.map(lambda _: VMEM, outs)
    return pl.pallas_call(
        kernel,
        out_shape=outs,
        in_specs=specs,
        out_specs=out_specs,
        scratch_shapes=list(scratch),
        compiler_params=pltpu.CompilerParams(vmem_limit_bytes=limit * 1024 * 1024),
        cost_estimate=pl.CostEstimate(flops=flops, bytes_accessed=1 << 20, transcendentals=0),
    )(*args)


def shape(dims, dtype):
    return jax.ShapeDtypeStruct(dims, dtype)


def iota(dims, axis):
    return lax.broadcasted_iota(jnp.int32, dims, axis)


def spreader(groups):
    return (iota((groups, C), 1) // GROUP == iota((groups, C), 0)).astype(F32).astype(BF)


def dequantized(codes, scales, spread):
    return codes.astype(F32) * jnp.dot(scales, spread, preferred_element_type=F32)


def fetch_kernel(asked_ref, codes_hbm, scales_hbm, out_ref, codes_ref, scales_ref, sems):
    senders, cap = asked_ref.shape
    rows, groups = scales_ref.shape
    stride = rows // cap
    part = 256
    copies = [pltpu.make_async_copy(scales_hbm, scales_ref, sems.at[0])]
    for at in range(rows // 512):
        block = pl.ds(at * 512, 512)
        copies.append(
            pltpu.make_async_copy(codes_hbm.at[block], codes_ref.at[block], sems.at[at + 1])
        )
    for copy in copies:
        copy.start()
    asked = asked_ref[...].astype(F32).astype(BF)
    targets = []
    for start in range(0, senders * cap, part):
        line = iota((part, senders), 0) + start
        pick = (line // cap == iota((part, senders), 1)).astype(F32).astype(BF)
        lists = jnp.dot(pick, asked, preferred_element_type=F32)
        entry = (iota((part, cap), 0) + start) % cap
        own = jnp.where(entry == iota((part, cap), 1), lists, 0.0)
        offset = jnp.sum(own, axis=1, keepdims=True).astype(jnp.int32)
        entry = (iota((part, 1), 0) + start) % cap
        targets.append(jnp.where(offset >= 0, entry * stride + offset, -1))
    spread = spreader(groups)
    for copy in copies:
        copy.wait()
    tables = []
    for start in range(0, rows, 256):
        block = pl.ds(start, 256)
        tables.append(dequantized(codes_ref[block, :], scales_ref[block, :], spread).astype(BF))
    table = jnp.concatenate(tables, axis=0)
    for at, target in enumerate(targets):
        chosen = (iota((part, rows), 1) == target).astype(F32).astype(BF)
        got = jnp.dot(chosen, table, preferred_element_type=F32)
        out_ref[pl.ds(at * part, part), :] = got.astype(BF)


def sigmoid(values):
    return 0.5 + 0.5 * jnp.tanh(0.5 * values)


def train_kernel(
    place_ref,
    slots_ref,
    code_ref,
    fetched_ref,
    weight_hbm,
    gain_ref,
    upstream_hbm,
    slot_grad_ref,
    keep_ref,
    send_ref,
    held_ref,
    conv_ref,
    unit_ref,
    scale_ref,
    grad_ref,
    wide_ref,
    weight_grad_ref,
    weight_ref,
    upstream_ref,
    sems,
):
    block = TAPS * C
    copies = [
        pltpu.make_async_copy(
            weight_hbm.at[pl.ds(layer * block, block)],
            weight_ref.at[pl.ds(layer * block, block)],
            sems.at[layer],
        )
        for layer in range(LAYERS)
    ]
    copies.append(pltpu.make_async_copy(upstream_hbm, upstream_ref, sems.at[LAYERS]))
    for copy in copies:
        copy.start()
    split, x, y, core = place_ref[0], place_ref[1], place_ref[2], place_ref[3]
    steps = range(0, PACKED, STEP)
    line = iota((PACKED, C), 0)
    since = jnp.where(line >= split, line - split, line)
    until = jnp.where(line >= split, PACKED - line, split - line)

    source = iota((PACKED, 1), 0)
    source = jnp.where(source >= split, source + (LEN - split), source)
    match = iota((PACKED, 2 * LEN), 1) == source
    packer = match.astype(F32).astype(BF)
    slot = jnp.where(match, slots_ref[...].astype(F32), 0.0)
    slot = jnp.sum(slot, axis=1, keepdims=True).astype(jnp.int32)
    slots = fetched_ref.shape[0]
    chosen = (iota((PACKED, slots), 1) == slot).astype(F32).astype(BF)
    first = jnp.dot(chosen, fetched_ref[...], preferred_element_type=F32)
    held_ref[0] = first.astype(BF)

    for layer in range(LAYERS):
        gap = DILATIONS[layer]
        now = held_ref[layer].astype(F32)
        taps = [held_ref[layer]]
        for tap in (1, 2):
            moved = pltpu.roll(now, tap * gap, 0)
            taps.append(jnp.where(since >= tap * gap, moved, 0.0).astype(BF))
        base = layer * TAPS * C
        copies[layer].wait()
        conv_ref[...] = jnp.dot(
            jnp.concatenate(taps, axis=1),
            weight_ref[pl.ds(base, TAPS * C), :],
            preferred_element_type=F32,
        )
        gain = gain_ref[pl.ds(layer, 1), :]
        for start in steps:
            part = pl.ds(start, STEP)
            value = conv_ref[part, :]
            center = value - jnp.mean(value, axis=1, keepdims=True)
            spread = jnp.mean(center * center, axis=1, keepdims=True)
            scale = lax.rsqrt(spread + 1e-5)
            unit = center * scale
            unit_ref[layer, part, :] = unit
            scale_ref[layer, part, :] = jnp.broadcast_to(scale, (STEP, 128))
            if layer + 1 < LAYERS:
                gained = unit * gain
                after = gained * sigmoid(gained)
                if layer % 2 == 1:
                    after = after + held_ref[layer - 1, part, :].astype(F32)
                held_ref[layer + 1, part, :] = after.astype(BF)

    copies[LAYERS].wait()
    grad_ref[...] = jnp.dot(packer, upstream_ref[...], preferred_element_type=F32)

    gain_rows = [None] * LAYERS
    for layer in reversed(range(LAYERS)):
        gap = DILATIONS[layer]
        gain = gain_ref[pl.ds(layer, 1), :]
        total = jnp.zeros((8, C), F32)
        for start in steps:
            part = pl.ds(start, STEP)
            unit = unit_ref[layer, part, :]
            scale = scale_ref[layer, part, :]
            gained = unit * gain
            gate = sigmoid(gained)
            inner = grad_ref[part, :] * (gate * (1.0 + gained * (1.0 - gate)))
            total = total + jnp.sum((inner * unit).reshape(STEP // 8, 8, C), axis=0)
            inner = inner * gain
            mean = jnp.mean(inner, axis=1, keepdims=True)
            slope = jnp.mean(inner * unit, axis=1, keepdims=True)
            outer = inner - mean - unit * slope
            conv_ref[part, :] = outer * jnp.concatenate([scale, scale], axis=1)
        gain_rows[layer] = jnp.sum(total, axis=0, keepdims=True)
        now = conv_ref[...]
        wide_ref[:, 0:C] = now.astype(BF)
        for tap in (1, 2):
            moved = pltpu.roll(now, PACKED - tap * gap, 0)
            moved = jnp.where(until > tap * gap, moved, 0.0)
            wide_ref[:, tap * C : (tap + 1) * C] = moved.astype(BF)

        below = jnp.zeros((PACKED, C), F32)
        for tap in range(TAPS):
            kernel = weight_ref[pl.ds((layer * TAPS + tap) * C, C), :]
            below = below + lax.dot_general(
                wide_ref[:, tap * C : (tap + 1) * C], kernel, NT, preferred_element_type=F32
            )
        if layer % 2 == 0:
            if layer == 2:
                skip = jnp.dot(packer, upstream_ref[...], preferred_element_type=F32)
            else:
                skip = held_ref[4].astype(F32)
            below = below + skip
        rounded = below.astype(BF)
        grad_ref[...] = rounded.astype(F32)
        if layer == 2:
            held_ref[4] = rounded

        weight_grad = lax.dot_general(
            held_ref[layer], wide_ref[...], TN, preferred_element_type=F32
        )
        for tap in range(TAPS):
            weight_grad_ref[pl.ds(tap * C, C), :] = weight_grad[:, tap * C : (tap + 1) * C]

        for pair in range(4):
            even = weight_grad_ref[pl.ds(2 * pair * PIECE, PIECE), :]
            odd = weight_grad_ref[pl.ds((2 * pair + 1) * PIECE, PIECE), :]
            tail = jnp.zeros((TAIL, C), F32)
            even_tail = tail
            if layer == 0 and pair == 0:
                exact = jnp.concatenate(gain_rows + gain_rows, axis=0)
                high = exact.astype(BF).astype(F32)
                even_tail = jnp.where(iota((TAIL, C), 0) < LAYERS, high, exact - high)
            even = jnp.concatenate([even, even_tail], axis=0)
            odd = jnp.concatenate([odd, tail], axis=0)
            place = ((layer - x + 4) % 4) * 4 + (pair - y + 4) % 4
            keep_ref[place] = jnp.where(core == 0, even, odd).astype(BF)
            send_ref[place] = jnp.where(core == 0, odd, even).astype(BF)

    mine = grad_ref[...].astype(BF)
    half = C // 2
    low = iota((32, 8, half), 1) < 4
    for start in range(0, slots, 256):
        here = iota((256, PACKED), 0) + start == code_ref[...]
        here = here.astype(F32).astype(BF)
        summed = jnp.dot(here, mine, preferred_element_type=F32)
        left = summed[:, :half].reshape(32, 8, half)
        right = summed[:, half:].reshape(32, 8, half)
        first = jnp.where(low, left, pltpu.roll(right, 4, 1))
        second = jnp.where(low, pltpu.roll(left, 4, 1), right)
        both = jnp.stack([first, second], axis=1).reshape(512, half)
        slot_grad_ref[pl.ds(2 * start, 512), :] = both.astype(BF)


def settle(total):
    tail = total[PIECE:SLAB, :]
    exact = tail + pltpu.roll(tail, LAYERS, 0)
    high = exact.astype(BF).astype(F32)
    tail = jnp.where(iota((TAIL, C), 0) < LAYERS, high, exact - high)
    return jnp.concatenate([total[:PIECE, :], tail], axis=0).astype(BF)


def core_sum_kernel(keep_ref, got_ref, *out_refs):
    for at in range(16):
        total = keep_ref[at].astype(F32) + got_ref[at].astype(F32)
        out_refs[at // 4][at % 4] = settle(total)


def four_sum_kernel(a_ref, b_ref, c_ref, d_ref, *out_refs):
    for at in range(a_ref.shape[0]):
        left = a_ref[at].astype(F32) + b_ref[at].astype(F32)
        right = c_ref[at].astype(F32) + d_ref[at].astype(F32)
        out_refs[at][0] = settle(left + right)


def merge_kernel(a_ref, b_ref, rows_ref, out_ref):
    slab = settle(a_ref[0].astype(F32) + b_ref[0].astype(F32)).astype(F32)
    out_ref[...] = jnp.concatenate([rows_ref[...].astype(F32), slab], axis=0).astype(BF)


def spread_kernel(count, plan, first, place_ref, *refs):
    sources, refs = refs[:count], refs[count:]
    if not first:
        gain_before, refs = refs[1], refs[2:]
    conv_hbm, gain_ref, refs = refs[0], refs[1], refs[2:]
    held, wide_ref, in_sems, out_sems = refs[:count], *refs[count:]
    x, y, core = place_ref[1], place_ref[2], place_ref[3]
    arrivals = [
        pltpu.make_async_copy(source, slot, in_sems.at[at])
        for at, (source, slot) in enumerate(zip(sources, held))
    ]
    for arrival in arrivals:
        arrival.start()
    gain_ref[...] = jnp.zeros_like(gain_ref) if first else gain_before[...]
    leaving = []
    ready = -1
    for at, (buffer, inner, along_x, along_y, other) in enumerate(plan):
        if buffer != ready:
            arrivals[buffer].wait()
            ready = buffer
        layer = (x + along_x) % 4
        side = core if other == 0 else 1 - core
        number = layer * 8 + ((y + along_y) % 4) * 2 + side
        if inner is None:
            block = held[buffer][...].astype(F32)[C:, :]
        else:
            block = held[buffer][inner].astype(F32)
        wide_ref[at] = block[:PIECE, :]
        copy = pltpu.make_async_copy(
            wide_ref.at[at],
            conv_hbm.at[pl.ds(pl.multiple_of(number * PIECE, PIECE), PIECE)],
            out_sems.at[at],
        )
        copy.start()
        leaving.append(copy)

        @pl.when(number == 0)
        def _():
            tail = block[PIECE:, :]
            gain_ref[...] = (tail + pltpu.roll(tail, LAYERS, 0))[:LAYERS, :]

    for copy in leaving:
        copy.wait()


def spread(place, blocks, plan, before=None):
    outs = [shape((LAYERS * TAPS * C, C), F32), shape((LAYERS, C), F32)]
    count = len(blocks)
    args, specs, aliases = [place] + blocks, [SMEM] + [ANY] * count, {}
    if before is not None:
        args, specs = args + list(before), specs + [HBM, VMEM]
        aliases = {count + 1: 0}
    return pl.pallas_call(
        functools.partial(spread_kernel, count, plan, before is None),
        out_shape=outs,
        in_specs=specs,
        out_specs=[HBM, VMEM],
        input_output_aliases=aliases,
        scratch_shapes=[pltpu.VMEM(block.shape, BF) for block in blocks]
        + [
            pltpu.VMEM((len(plan), PIECE, C), F32),
            pltpu.SemaphoreType.DMA((count,)),
            pltpu.SemaphoreType.DMA((len(plan),)),
        ],
        compiler_params=pltpu.CompilerParams(vmem_limit_bytes=8 * 1024 * 1024),
        cost_estimate=pl.CostEstimate(flops=0, bytes_accessed=1 << 21, transcendentals=0),
    )(*args)


def scatter_kernel(place_ref, code_a, code_b, code_c, code_d, got_ref, out_ref):
    y, core = place_ref[2], place_ref[3]
    own = y * 2 + core
    lines = code_a.shape[1]
    total = [jnp.zeros((C, C // 2), F32)] * 2
    for along, code_ref in enumerate((code_a, code_b, code_c, code_d)):
        for other in range(2):
            side = core if other == 0 else 1 - core
            group = ((y + along) % 4) * 2 + side
            code = code_ref[pl.ds(other * 8 + own, 1), :]
            got = got_ref[pl.ds(pl.multiple_of(group * lines, lines), lines), :]
            for half in range(2):
                here = iota((C, lines), 0) + half * C == code
                here = here.astype(F32).astype(BF)
                total[half] = total[half] + jnp.dot(here, got, preferred_element_type=F32)
    out_ref[...] = jnp.concatenate(total, axis=1).astype(BF)


def adagrad_kernel(place_ref, *refs):
    sources, (codes_hbm, scales_ref, accum_ref) = refs[:8], refs[8:11]
    rows_hbm, next_ref = refs[11:13]
    held, codes_ref, rows_ref, in_sems, table_sems, out_sems = refs[13:21], *refs[21:]
    spread = spreader(scales_ref.shape[1])
    y, core = place_ref[2], place_ref[3]
    arrivals, tables, leaving = [], [], []
    for at in range(8):
        copy = pltpu.make_async_copy(sources[at], held[at], in_sems.at[at])
        copy.start()
        arrivals.append(copy)
        side = core if at < 4 else 1 - core
        number = ((y + at % 4) % 4) * 2 + side
        part = pl.ds(pl.multiple_of(number * C, C), C)
        copy = pltpu.make_async_copy(codes_hbm.at[part], codes_ref.at[at], table_sems.at[at])
        copy.start()
        tables.append((copy, number, part))
    same = iota((C, C), 0) == iota((C, C), 1)
    for at in range(8):
        copy, number, part = tables[at]
        arrivals[at].wait()
        copy.wait()
        gradient = held[at][...].astype(F32)[:C, :]
        grown = accum_ref[part, :] + jnp.mean(gradient * gradient, axis=1, keepdims=True)
        table = dequantized(codes_ref[at], scales_ref[part, :], spread)
        rows_ref[at] = table - LEARN_RATE * gradient * lax.rsqrt(grown)
        copy = pltpu.make_async_copy(rows_ref.at[at], rows_hbm.at[part], out_sems.at[at])
        copy.start()
        leaving.append(copy)
        next_ref[pl.ds(number, 1), :] = jnp.sum(
            jnp.where(same, grown, 0.0), axis=0, keepdims=True
        )
    for copy in leaving:
        copy.wait()


def shifted(values, axis, size, offset):
    return lax.ppermute(values, axis, [(i, (i + offset) % size) for i in range(size)])


def crossed(values, axis, size, bits):
    return lax.ppermute(values, axis, [(i, i ^ bits) for i in range(size)])


def body(lengths, slots, requests, counts, codes, scales, accum, conv_weight, norm_gain, upstream):
    table_axes = ("x", "z")
    owners = requests.shape[1]
    cap = requests.shape[2]
    rows = codes.shape[0]
    stride = rows // cap
    split = lengths[0, 0]
    place = jnp.stack(
        [split, lax.axis_index("x"), lax.axis_index("y"), lax.axis_index("core")]
    ).astype(jnp.int32)

    y, core = lax.axis_index("y"), lax.axis_index("core")

    entry = jnp.arange(cap, dtype=jnp.int32)[None, :]
    wanted = jnp.where(entry < counts[0][:, None], requests[0] - entry * stride, -1)
    asked = lax.all_to_all(wanted, table_axes, split_axis=0, concat_axis=0, tiled=True)

    order = jnp.arange(PACKED, dtype=jnp.int32)
    order = order + jnp.where(order >= split, LEN - split, 0)
    match = order[:, None] == jnp.arange(2 * LEN, dtype=jnp.int32)[None, :]
    packed = jnp.sum(jnp.where(match, slots.reshape(1, 2 * LEN), 0), axis=1)
    each = cap // 8
    code = (packed % cap) // each * (owners * each) + packed // cap * each + packed % each

    sending = call(
        fetch_kernel,
        shape((owners * cap, C), BF),
        [asked, codes, scales],
        specs=[VMEM, HBM, HBM],
        scratch=[
            pltpu.VMEM((rows, C), BF),
            pltpu.VMEM(scales.shape, BF),
            pltpu.SemaphoreType.DMA((rows // 512 + 1,)),
        ],
        flops=1 << 30,
        limit=16,
    )
    fetched = lax.all_to_all(
        sending.reshape(owners, cap, C), table_axes, split_axis=0, concat_axis=0, tiled=True
    ).reshape(owners * cap, C)

    lists = asked.reshape(owners, 8, each).transpose(1, 0, 2)[:, :, None, :]
    base = jnp.arange(2, dtype=jnp.int32)[:, None] * C
    base = base + jnp.arange(each, dtype=jnp.int32)[None, :] * stride
    target = jnp.where(lists >= 0, lists + base, -1).reshape(8, 2 * owners * each)
    target = jnp.concatenate([target, crossed(target, "core", 2, 1)], axis=0)
    targets = [target] + [shifted(target, "y", 4, -k) for k in (1, 2, 3)]
    fetched, *targets = lax.optimization_barrier((fetched, *targets))

    slab16 = shape((16, SLAB, C), BF)
    slot_grad, keep, send = call(
        train_kernel,
        [shape((2 * owners * cap, C // 2), BF), slab16, slab16],
        [
            place,
            slots.reshape(1, 2 * LEN),
            code.reshape(1, PACKED),
            fetched,
            conv_weight.reshape(LAYERS * TAPS * C, C),
            norm_gain,
            upstream.reshape(2 * LEN, C),
        ],
        specs=[SMEM, VMEM, VMEM, VMEM, HBM, VMEM, HBM],
        scratch=[
            pltpu.VMEM((LAYERS + 1, PACKED, C), BF),
            pltpu.VMEM((PACKED, C), F32),
            pltpu.VMEM((LAYERS, PACKED, C), F32),
            pltpu.VMEM((LAYERS, PACKED, 128), F32),
            pltpu.VMEM((PACKED, C), F32),
            pltpu.VMEM((PACKED, TAPS * C), BF),
            pltpu.VMEM((TAPS * C, C), F32),
            pltpu.VMEM((LAYERS * TAPS * C, C), BF),
            pltpu.VMEM((2 * LEN, C), BF),
            pltpu.SemaphoreType.DMA((LAYERS + 1,)),
        ],
        flops=1 << 32,
        limit=24,
    )

    got = crossed(send, "core", 2, 1)
    slab4, slab1 = shape((4, SLAB, C), BF), shape((1, SLAB, C), BF)
    parts = call(core_sum_kernel, [slab4] * 4, [keep, got])
    slot_grad, *parts = lax.optimization_barrier((slot_grad, *parts))
    returned = lax.all_to_all(
        slot_grad.reshape(8 * owners, 8, C // 2),
        ("y", "core", "x", "z"),
        split_axis=0,
        concat_axis=0,
        tiled=True,
    ).reshape(2 * owners * cap, C // 2)
    parts = [parts[0]] + [shifted(parts[k], "x", 4, k) for k in (1, 2, 3)]
    parts = call(four_sum_kernel, [slab1] * 4, parts)
    parts = [parts[0]] + [shifted(parts[k], "y", 4, k) for k in (1, 2, 3)]
    (part,) = call(four_sum_kernel, [slab1], parts)
    (part,) = call(
        four_sum_kernel, [slab1], [part] + [crossed(part, "z", 8, k) for k in (1, 2, 3)]
    )
    other = crossed(part, "z", 8, 6)
    part, returned = lax.optimization_barrier((part, returned))
    mine = call(
        scatter_kernel,
        shape((C, C), BF),
        [place] + targets + [returned],
        specs=[SMEM] + [VMEM] * 5,
        flops=1 << 30,
    )
    merged = call(merge_kernel, shape((C + SLAB, C), BF), [part, other, mine])
    merged = [merged] + [shifted(merged, "y", 4, -k) for k in (1, 2, 3)]
    across = [crossed(block, "core", 2, 1) for block in merged]
    parts = jnp.stack([block[C:] for block in merged])
    later = [shifted(parts, "x", 4, -k) for k in (1, 2, 3)]
    blocks = pltpu.VMEM((C + SLAB, C), BF)
    new_rows, next_accum = call(
        adagrad_kernel,
        [shape((rows, C), F32), shape((8, C), F32)],
        [place] + merged + across + [codes, scales, accum.reshape(rows, 1)],
        specs=[SMEM] + [ANY] * 8 + [HBM, VMEM, VMEM],
        out_specs=[HBM, VMEM],
        scratch=[blocks] * 8
        + [
            pltpu.VMEM((8, C, C), BF),
            pltpu.VMEM((8, C, C), F32),
            pltpu.SemaphoreType.DMA((8,)),
            pltpu.SemaphoreType.DMA((8,)),
            pltpu.SemaphoreType.DMA((8,)),
        ],
        limit=12,
    )
    here = [(at, None, 0, at, 0) for at in range(4)]
    here += [(4 + at, None, 0, at, 1) for at in range(4)]
    filled = spread(place, merged + across, here)
    later, next_accum, filled = lax.optimization_barrier((later, next_accum, filled))
    beyond = [crossed(part, "core", 2, 1) for part in later]
    plan = [(at, inner, at + 1, inner, 0) for at in range(3) for inner in range(4)]
    filled = spread(place, later, plan, filled)
    plan = [(at, inner, at + 1, inner, 1) for at in range(3) for inner in range(4)]
    grad_conv, grad_gain = spread(place, beyond, plan, filled)
    return (
        new_rows,
        next_accum.reshape(rows),
        grad_conv.reshape(conv_weight.shape),
        grad_gain,
    )


def solution(mesh):
    fine = Mesh(mesh.devices.reshape(4, 8, 4, 2), ("x", "z", "y", "core"))
    every = ("x", "z", "y", "core")
    table = ("x", "z")
    return jax.shard_map(
        body,
        mesh=fine,
        in_specs=(
            P(every, None),
            P(every, None),
            P(every, None, None),
            P(every, None),
            P(table, None),
            P(table, None),
            P(table),
            P(),
            P(),
            P(every, None, None),
        ),
        out_specs=(P(table, None), P(table), P(), P()),
        check_vma=False,
    )
```

```python
import functools

import jax
import jax.numpy as jnp
from jax import lax
from jax.experimental import pallas as pl
from jax.experimental.pallas import tpu as pltpu
from jax.sharding import Mesh
from jax.sharding import PartitionSpec as P

DILATIONS = (1, 2, 4, 8)
LEARN_RATE = 0.5
BF = jnp.bfloat16
F32 = jnp.float32
LAYERS, TAPS, C = 4, 3, 256
GROUP = 32
LEN = 256
PACKED = 320
STEP = 64
PIECE = 96
TAIL = 8
SLAB = PIECE + TAIL
NT = (((1,), (1,)), ((), ()))
TN = (((0,), (0,)), ((), ()))
SMEM = pl.BlockSpec(memory_space=pltpu.SMEM)
VMEM = pl.BlockSpec(memory_space=pltpu.VMEM)
ANY = pl.BlockSpec(memory_space=pl.ANY)
HBM = pl.BlockSpec(memory_space=pltpu.HBM)


def call(kernel, outs, args, specs=None, out_specs=None, scratch=(), flops=0, limit=8):
    if specs is None:
        specs = [VMEM] * len(args)
    if out_specs is None:
        out_specs = jax.tree.map(lambda _: VMEM, outs)
    return pl.pallas_call(
        kernel,
        out_shape=outs,
        in_specs=specs,
        out_specs=out_specs,
        scratch_shapes=list(scratch),
        compiler_params=pltpu.CompilerParams(vmem_limit_bytes=limit * 1024 * 1024),
        cost_estimate=pl.CostEstimate(flops=flops, bytes_accessed=1 << 20, transcendentals=0),
    )(*args)


def shape(dims, dtype):
    return jax.ShapeDtypeStruct(dims, dtype)


def iota(dims, axis):
    return lax.broadcasted_iota(jnp.int32, dims, axis)


def spreader(groups):
    return (iota((groups, C), 1) // GROUP == iota((groups, C), 0)).astype(F32).astype(BF)


def dequantized(codes, scales, spread):
    return codes.astype(F32) * jnp.dot(scales, spread, preferred_element_type=F32)


def table_kernel(codes_ref, scales_ref, table_ref):
    spread = spreader(scales_ref.shape[1])
    for start in range(0, codes_ref.shape[0], 256):
        part = pl.ds(start, 256)
        table = dequantized(codes_ref[part, :], scales_ref[part, :], spread)
        table_ref[part, :] = table.astype(BF)


def fetch_kernel(asked_ref, table_ref, out_ref):
    senders, cap = asked_ref.shape
    stride = table_ref.shape[0] // cap
    asked = asked_ref[...].astype(F32).astype(BF)
    part, width = 8 * senders, 8 * stride
    pick = (iota((part, senders), 0) // 8 == iota((part, senders), 1)).astype(F32).astype(BF)
    lists = jnp.dot(pick, asked, preferred_element_type=F32)
    entry = iota((part, 1), 0) % 8
    halves = []
    for at in range(cap // 8):
        own = iota((part, cap), 1) == iota((part, cap), 0) % 8 + at * 8
        offset = jnp.sum(jnp.where(own, lists, 0.0), axis=1, keepdims=True).astype(jnp.int32)
        target = jnp.where(offset >= 0, entry * stride + offset, -1)
        chosen = (iota((part, width), 1) == target).astype(F32).astype(BF)
        got = jnp.dot(chosen, table_ref[pl.ds(at * width, width), :], preferred_element_type=F32)
        halves.append(got.reshape(senders, 8, C))
        if at % 2 == 1:
            both = jnp.concatenate(halves, axis=1)
            out_ref[:, pl.ds((at - 1) * 8, 16), :] = both.astype(BF)
            halves = []


def sigmoid(values):
    return 0.5 + 0.5 * jnp.tanh(0.5 * values)


def train_kernel(
    place_ref,
    slots_ref,
    code_ref,
    fetched_ref,
    gain_ref,
    upstream_ref,
    *refs,
):
    weight_refs, refs = refs[: LAYERS * TAPS], refs[LAYERS * TAPS :]
    slot_grad_ref, keep_ref, send_ref, held_ref, conv_ref, unit_ref = refs[:6]
    scale_ref, grad_ref, wide_ref, weight_grad_ref = refs[6:]
    split, x, y, core = place_ref[0], place_ref[1], place_ref[2], place_ref[3]
    steps = range(0, PACKED, STEP)
    line = iota((PACKED, C), 0)
    since = jnp.where(line >= split, line - split, line)
    until = jnp.where(line >= split, PACKED - line, split - line)

    source = iota((PACKED, 1), 0)
    source = jnp.where(source >= split, source + (LEN - split), source)
    match = iota((PACKED, 2 * LEN), 1) == source
    packer = match.astype(F32).astype(BF)
    slot = jnp.where(match, slots_ref[...].astype(F32), 0.0)
    slot = jnp.sum(slot, axis=1, keepdims=True).astype(jnp.int32)
    slots = fetched_ref.shape[0]
    chosen = (iota((PACKED, slots), 1) == slot).astype(F32).astype(BF)
    first = jnp.dot(chosen, fetched_ref[...], preferred_element_type=F32)
    held_ref[0] = first.astype(BF)

    for layer in range(LAYERS):
        gap = DILATIONS[layer]
        now = held_ref[layer].astype(F32)
        taps = [held_ref[layer]]
        for tap in (1, 2):
            moved = pltpu.roll(now, tap * gap, 0)
            taps.append(jnp.where(since >= tap * gap, moved, 0.0).astype(BF))
        conv_ref[...] = jnp.dot(
            jnp.concatenate(taps, axis=1),
            jnp.concatenate([ref[...] for ref in weight_refs[layer * TAPS :][:TAPS]], axis=0),
            preferred_element_type=F32,
        )
        gain = gain_ref[pl.ds(layer, 1), :]
        for start in steps:
            part = pl.ds(start, STEP)
            value = conv_ref[part, :]
            center = value - jnp.mean(value, axis=1, keepdims=True)
            spread = jnp.mean(center * center, axis=1, keepdims=True)
            scale = lax.rsqrt(spread + 1e-5)
            unit = center * scale
            unit_ref[layer, part, :] = unit
            scale_ref[layer, part, :] = jnp.broadcast_to(scale, (STEP, 128))
            if layer + 1 < LAYERS:
                gained = unit * gain
                after = gained * sigmoid(gained)
                if layer % 2 == 1:
                    after = after + held_ref[layer - 1, part, :].astype(F32)
                held_ref[layer + 1, part, :] = after.astype(BF)

    upstream = jnp.dot(packer, upstream_ref[...], preferred_element_type=F32)
    grad_ref[...] = upstream
    held_ref[5] = upstream.astype(BF)

    gain_rows = [None] * LAYERS
    for layer in reversed(range(LAYERS)):
        gap = DILATIONS[layer]
        gain = gain_ref[pl.ds(layer, 1), :]
        total = jnp.zeros((8, C), F32)
        for start in steps:
            part = pl.ds(start, STEP)
            unit = unit_ref[layer, part, :]
            scale = scale_ref[layer, part, :]
            gained = unit * gain
            gate = sigmoid(gained)
            inner = grad_ref[part, :] * (gate * (1.0 + gained * (1.0 - gate)))
            total = total + jnp.sum((inner * unit).reshape(STEP // 8, 8, C), axis=0)
            inner = inner * gain
            mean = jnp.mean(inner, axis=1, keepdims=True)
            slope = jnp.mean(inner * unit, axis=1, keepdims=True)
            outer = inner - mean - unit * slope
            conv_ref[part, :] = outer * jnp.concatenate([scale, scale], axis=1)
        gain_rows[layer] = jnp.sum(total, axis=0, keepdims=True)
        now = conv_ref[...]
        wide_ref[:, 0:C] = now.astype(BF)
        for tap in (1, 2):
            moved = pltpu.roll(now, PACKED - tap * gap, 0)
            moved = jnp.where(until > tap * gap, moved, 0.0)
            wide_ref[:, tap * C : (tap + 1) * C] = moved.astype(BF)

        below = jnp.zeros((PACKED, C), F32)
        for tap in range(TAPS):
            kernel = weight_refs[layer * TAPS + tap][...]
            below = below + lax.dot_general(
                wide_ref[:, tap * C : (tap + 1) * C], kernel, NT, preferred_element_type=F32
            )
        if layer % 2 == 0:
            if layer == 2:
                skip = held_ref[5].astype(F32)
            else:
                skip = held_ref[4].astype(F32)
            below = below + skip
        rounded = below.astype(BF)
        grad_ref[...] = rounded.astype(F32)
        if layer == 2:
            held_ref[4] = rounded

        weight_grad = lax.dot_general(
            held_ref[layer], wide_ref[...], TN, preferred_element_type=F32
        )
        for tap in range(TAPS):
            weight_grad_ref[pl.ds(tap * C, C), :] = weight_grad[:, tap * C : (tap + 1) * C]

        for pair in range(4):
            even = weight_grad_ref[pl.ds(2 * pair * PIECE, PIECE), :]
            odd = weight_grad_ref[pl.ds((2 * pair + 1) * PIECE, PIECE), :]
            tail = jnp.zeros((TAIL, C), F32)
            even_tail = tail
            if layer == 0 and pair == 0:
                exact = jnp.concatenate(gain_rows + gain_rows, axis=0)
                high = exact.astype(BF).astype(F32)
                even_tail = jnp.where(iota((TAIL, C), 0) < LAYERS, high, exact - high)
            even = jnp.concatenate([even, even_tail], axis=0)
            odd = jnp.concatenate([odd, tail], axis=0)
            place = ((pair - y + 4) % 4) * 4 + (layer - x + 4) % 4
            keep_ref[place] = jnp.where(core == 0, even, odd).astype(BF)
            send_ref[place] = jnp.where(core == 0, odd, even).astype(BF)

    mine = grad_ref[...].astype(BF)
    for start in range(0, slots, 256):
        here = iota((256, PACKED), 0) + start == code_ref[...]
        here = here.astype(F32).astype(BF)
        summed = jnp.dot(here, mine, preferred_element_type=F32)
        slot_grad_ref[pl.ds(start, 256), :] = summed.astype(BF)


def settle(total):
    tail = total[PIECE:SLAB, :]
    exact = tail + pltpu.roll(tail, LAYERS, 0)
    high = exact.astype(BF).astype(F32)
    tail = jnp.where(iota((TAIL, C), 0) < LAYERS, high, exact - high)
    return jnp.concatenate([total[:PIECE, :], tail], axis=0).astype(BF)


def core_sum_kernel(keep_ref, got_ref, *out_refs):
    for at in range(16):
        total = keep_ref[at].astype(F32) + got_ref[at].astype(F32)
        out_refs[at // 4][at % 4] = settle(total)


def four_sum_kernel(a_ref, b_ref, c_ref, d_ref, *out_refs):
    for at in range(a_ref.shape[0]):
        left = a_ref[at].astype(F32) + b_ref[at].astype(F32)
        right = c_ref[at].astype(F32) + d_ref[at].astype(F32)
        out_refs[at][0] = settle(left + right)


def last_sum_kernel(a_ref, b_ref, *refs):
    slab = settle(a_ref[0].astype(F32) + b_ref[0].astype(F32)).astype(F32)
    rows = refs[0][0].astype(F32) + refs[1][0].astype(F32)
    refs[2][...] = jnp.concatenate([rows, slab], axis=0).astype(BF)


def part_kernel(*refs):
    for at, ref in enumerate(refs[:4]):
        both = ref[...].astype(F32)
        refs[4][at] = both[:C].astype(BF)
        refs[5][at] = both[C:].astype(BF)


def spread_kernel(count, plan, first, place_ref, *refs):
    sources, refs = refs[:count], refs[count:]
    if not first:
        gain_before, refs = refs[1], refs[2:]
    conv_hbm, gain_ref, wide_ref, sems = refs
    x, y, core = place_ref[1], place_ref[2], place_ref[3]
    gain_ref[...] = jnp.zeros_like(gain_ref) if first else gain_before[...]
    leaving = []
    for at, (buffer, inner, along_x, along_y, other) in enumerate(plan):
        layer = (x + along_x) % 4
        side = core if other == 0 else 1 - core
        number = layer * 8 + ((y + along_y) % 4) * 2 + side
        block = sources[buffer][inner].astype(F32)
        wide_ref[at] = block[:PIECE, :]
        copy = pltpu.make_async_copy(
            wide_ref.at[at],
            conv_hbm.at[pl.ds(pl.multiple_of(number * PIECE, PIECE), PIECE)],
            sems.at[at],
        )
        copy.start()
        leaving.append(copy)

        @pl.when(number == 0)
        def _():
            tail = block[PIECE:, :]
            gain_ref[...] = (tail + pltpu.roll(tail, LAYERS, 0))[:LAYERS, :]

    for copy in leaving:
        copy.wait()


def spread(place, blocks, plan, before=None):
    outs = [shape((LAYERS * TAPS * C, C), F32), shape((LAYERS, C), F32)]
    count = len(blocks)
    args, specs, aliases = [place] + blocks, [SMEM] + [VMEM] * count, {}
    if before is not None:
        args, specs = args + list(before), specs + [HBM, VMEM]
        aliases = {count + 1: 0}
    return pl.pallas_call(
        functools.partial(spread_kernel, count, plan, before is None),
        out_shape=outs,
        in_specs=specs,
        out_specs=[HBM, VMEM],
        input_output_aliases=aliases,
        scratch_shapes=[
            pltpu.VMEM((len(plan), PIECE, C), F32),
            pltpu.SemaphoreType.DMA((len(plan),)),
        ],
        compiler_params=pltpu.CompilerParams(vmem_limit_bytes=8 * 1024 * 1024),
        cost_estimate=pl.CostEstimate(flops=0, bytes_accessed=1 << 21, transcendentals=0),
    )(*args)


def scatter_kernel(place_ref, code_ref, got_ref, keep_ref, send_ref):
    y, core = place_ref[2], place_ref[3]
    senders = got_ref.shape[0]
    lines = code_ref.shape[1]
    for pair in range(4):
        if pair % 2 == 0:
            both = got_ref[:, pl.ds(pair * 8, 16), :].astype(F32).reshape(senders, 2, 8, C)
        got = both[:, pair % 2].reshape(lines, C).astype(BF)
        here = iota((2 * C, lines), 0) + pair * 2 * C == code_ref[pl.ds(pair, 1), :]
        here = here.astype(F32).astype(BF)
        total = jnp.dot(here, got, preferred_element_type=F32)
        even, odd = total[:C], total[C:]
        apart = pair ^ y
        place = jnp.where(apart == 3, 1, jnp.where(apart == 0, 0, apart + 1))
        keep_ref[place] = jnp.where(core == 0, even, odd).astype(BF)
        send_ref[place] = jnp.where(core == 0, odd, even).astype(BF)


def row_sum_kernel(keep_ref, got_ref, *out_refs):
    half = keep_ref.shape[0] // 2
    total = (keep_ref[...].astype(F32) + got_ref[...].astype(F32)).astype(BF)
    out_refs[0][...] = total[:half]
    out_refs[1][...] = total[half:]


def adagrad_kernel(place_ref, *refs):
    own_ref, across_ref, codes_ref, scales_ref, accum_ref = refs[:5]
    rows_hbm, next_ref, rows_ref, sems = refs[5:]
    spread = spreader(scales_ref.shape[1])
    y, core = place_ref[2], place_ref[3]
    same = iota((C, C), 0) == iota((C, C), 1)
    half = C // 2
    leaving = []
    for at in range(8):
        side = core if at < 4 else 1 - core
        number = ((y + at % 4) % 4) * 2 + side
        part = pl.ds(pl.multiple_of(number * C, C), C)
        gradient = (own_ref[at] if at < 4 else across_ref[at - 4]).astype(F32)
        lines = [accum_ref[pl.ds(2 * number + side, 1), :] for side in range(2)]
        line = jnp.concatenate(lines, axis=1)
        grown = jnp.sum(jnp.where(same, line, 0.0), axis=1, keepdims=True)
        grown = grown + jnp.mean(gradient * gradient, axis=1, keepdims=True)
        table = dequantized(codes_ref[part, :], scales_ref[part, :], spread)
        rows_ref[at] = table - LEARN_RATE * gradient * lax.rsqrt(grown)
        copy = pltpu.make_async_copy(rows_ref.at[at], rows_hbm.at[part], sems.at[at])
        copy.start()
        leaving.append(copy)
        line = jnp.sum(jnp.where(same, grown, 0.0), axis=0, keepdims=True)
        next_ref[pl.ds(2 * number, 1), :] = line[:, :half]
        next_ref[pl.ds(2 * number + 1, 1), :] = line[:, half:]
    for copy in leaving:
        copy.wait()


def shifted(values, axis, size, offset):
    return lax.ppermute(values, axis, [(i, (i + offset) % size) for i in range(size)])


def crossed(values, axis, size, bits):
    return lax.ppermute(values, axis, [(i, i ^ bits) for i in range(size)])


def after(values, *others):
    return lax.optimization_barrier((values, *others))[0]


def body(lengths, slots, requests, counts, codes, scales, accum, conv_weight, norm_gain, upstream):
    table_axes = ("x", "z")
    owners = requests.shape[1]
    cap = requests.shape[2]
    rows = codes.shape[0]
    stride = rows // cap
    split = lengths[0, 0]
    place = jnp.stack(
        [split, lax.axis_index("x"), lax.axis_index("y"), lax.axis_index("core")]
    ).astype(jnp.int32)

    entry = jnp.arange(cap, dtype=jnp.int32)[None, :]
    wanted = jnp.where(entry < counts[0][:, None], requests[0] - entry * stride, -1)
    asked = lax.all_to_all(wanted, table_axes, split_axis=0, concat_axis=0, tiled=True)

    order = jnp.arange(PACKED, dtype=jnp.int32)
    order = order + jnp.where(order >= split, LEN - split, 0)
    match = order[:, None] == jnp.arange(2 * LEN, dtype=jnp.int32)[None, :]
    packed = jnp.sum(jnp.where(match, slots.reshape(1, 2 * LEN), 0), axis=1)

    table = call(table_kernel, shape((rows, C), BF), [codes, scales], flops=1 << 24)
    sending = call(
        fetch_kernel, shape((owners, cap, C), BF), [asked, table], flops=1 << 30
    )
    fetched = lax.all_to_all(
        sending, table_axes, split_axis=0, concat_axis=0, tiled=True
    ).reshape(owners * cap, C)

    target = jnp.where(asked >= 0, asked + entry * stride, -1)
    target = target.reshape(owners, 4, 8).transpose(1, 0, 2).reshape(4, 8 * owners)
    fetched, target = lax.optimization_barrier((fetched, target))

    slab16 = shape((16, SLAB, C), BF)
    slot_grad, keep, send = call(
        train_kernel,
        [shape((owners * cap, C), BF), slab16, slab16],
        [
            place,
            slots.reshape(1, 2 * LEN),
            packed.reshape(1, PACKED),
            fetched,
            norm_gain,
            upstream.reshape(2 * LEN, C),
            *[conv_weight[layer, tap] for layer in range(LAYERS) for tap in range(TAPS)],
        ],
        specs=[SMEM] + [VMEM] * 17,
        scratch=[
            pltpu.VMEM((LAYERS + 2, PACKED, C), BF),
            pltpu.VMEM((PACKED, C), F32),
            pltpu.VMEM((LAYERS, PACKED, C), F32),
            pltpu.VMEM((LAYERS, PACKED, 128), F32),
            pltpu.VMEM((PACKED, C), F32),
            pltpu.VMEM((PACKED, TAPS * C), BF),
            pltpu.VMEM((TAPS * C, C), F32),
        ],
        flops=1 << 32,
        limit=16,
    )

    got = crossed(send, "core", 2, 1)
    returned = lax.all_to_all(
        slot_grad.reshape(owners, cap, C), table_axes, split_axis=0, concat_axis=0, tiled=True
    )
    slab4, slab1 = shape((4, SLAB, C), BF), shape((1, SLAB, C), BF)
    block4 = shape((4, C, C), BF)

    parts = call(core_sum_kernel, [slab4] * 4, [keep, got])
    parts = [parts[0]] + [shifted(parts[k], "y", 4, k) for k in (1, 2, 3)]
    parts = call(four_sum_kernel, [slab1] * 4, parts)
    keep_rows, send_rows = call(
        scatter_kernel,
        [block4, block4],
        [place, target, after(returned, parts[0])],
        specs=[SMEM, VMEM, VMEM],
        flops=1 << 29,
    )
    parts = [parts[0]] + [shifted(parts[k], "x", 4, k) for k in (1, 2, 3)]
    sums = [keep_rows, crossed(send_rows, "core", 2, 1)]
    parts, sums = lax.optimization_barrier((parts, sums))

    (part,) = call(four_sum_kernel, [slab1], parts)
    keep_rows, send_rows = call(row_sum_kernel, [shape((2, C, C), BF)] * 2, sums)
    parts = [part] + [crossed(part, "z", 8, k) for k in (1, 2, 3)]
    sums = [keep_rows, crossed(send_rows, "y", 4, 1)]
    parts, sums = lax.optimization_barrier((parts, sums))
    (part,) = call(four_sum_kernel, [slab1], parts)
    keep_rows, send_rows = call(row_sum_kernel, [shape((1, C, C), BF)] * 2, sums)
    parts = [part, crossed(part, "z", 8, 6)]
    sums = [keep_rows, crossed(send_rows, "y", 4, 3)]
    parts, sums = lax.optimization_barrier((parts, sums))

    part = call(last_sum_kernel, shape((C + SLAB, C), BF), parts + sums)
    parts = [part] + [shifted(part, "y", 4, -k) for k in (1, 2, 3)]
    mine, parts = call(part_kernel, [block4, slab4], parts)
    later = [shifted(parts, "x", 4, -k) for k in (1, 2, 3)]
    across = crossed(mine, "core", 2, 1)
    new_rows, next_accum = call(
        adagrad_kernel,
        [shape((rows, C), F32), shape((rows // 128, 128), F32)],
        [place, mine, across, codes, scales, accum.reshape(rows // 128, 128)],
        specs=[SMEM] + [VMEM] * 5,
        out_specs=[HBM, VMEM],
        scratch=[pltpu.VMEM((8, C, C), F32), pltpu.SemaphoreType.DMA((8,))],
    )
    later = after(later, next_accum)
    held = [parts] + later
    plan = [(at, inner, at, inner, 0) for at in range(4) for inner in range(4)]
    filled = spread(place, held, plan)
    plan = [(at, inner, at, inner, 1) for at in range(4) for inner in range(4)]
    beyond = [crossed(part, "core", 2, 1) for part in held]
    grad_conv, grad_gain = spread(place, beyond, plan, filled)
    return (
        new_rows,
        next_accum.reshape(rows),
        grad_conv.reshape(conv_weight.shape),
        grad_gain,
    )


def solution(mesh):
    fine = Mesh(mesh.devices.reshape(4, 8, 4, 2), ("x", "z", "y", "core"))
    every = ("x", "z", "y", "core")
    table = ("x", "z")
    return jax.shard_map(
        body,
        mesh=fine,
        in_specs=(
            P(every, None),
            P(every, None),
            P(every, None, None),
            P(every, None),
            P(table, None),
            P(table, None),
            P(table),
            P(),
            P(),
            P(every, None, None),
        ),
        out_specs=(P(table, None), P(table), P(), P()),
        check_vma=False,
    )
```

```python
import functools

import jax
import jax.numpy as jnp
from jax import lax
from jax.experimental import pallas as pl
from jax.experimental.pallas import tpu as pltpu
from jax.sharding import Mesh
from jax.sharding import PartitionSpec as P

DILATIONS = (1, 2, 4, 8)
LEARN_RATE = 0.5
BF = jnp.bfloat16
F32 = jnp.float32
LAYERS, TAPS, C = 4, 3, 256
GROUP = 32
LEN = 256
PACKED = 320
STEP = 64
PIECE = 96
TAIL = 8
SLAB = PIECE + TAIL
NT = (((1,), (1,)), ((), ()))
TN = (((0,), (0,)), ((), ()))
SMEM = pl.BlockSpec(memory_space=pltpu.SMEM)
VMEM = pl.BlockSpec(memory_space=pltpu.VMEM)
ANY = pl.BlockSpec(memory_space=pl.ANY)
HBM = pl.BlockSpec(memory_space=pltpu.HBM)


def call(kernel, outs, args, specs=None, out_specs=None, scratch=(), flops=0, limit=8):
    if specs is None:
        specs = [VMEM] * len(args)
    if out_specs is None:
        out_specs = jax.tree.map(lambda _: VMEM, outs)
    return pl.pallas_call(
        kernel,
        out_shape=outs,
        in_specs=specs,
        out_specs=out_specs,
        scratch_shapes=list(scratch),
        compiler_params=pltpu.CompilerParams(vmem_limit_bytes=limit * 1024 * 1024),
        cost_estimate=pl.CostEstimate(flops=flops, bytes_accessed=1 << 20, transcendentals=0),
    )(*args)


def shape(dims, dtype):
    return jax.ShapeDtypeStruct(dims, dtype)


def iota(dims, axis):
    return lax.broadcasted_iota(jnp.int32, dims, axis)


def spreader(groups):
    return (iota((groups, C), 1) // GROUP == iota((groups, C), 0)).astype(F32).astype(BF)


def dequantized(codes, scales, spread):
    return codes.astype(F32) * jnp.dot(scales, spread, preferred_element_type=F32)


def table_kernel(codes_ref, scales_ref, table_ref):
    spread = spreader(scales_ref.shape[1])
    for start in range(0, codes_ref.shape[0], 256):
        part = pl.ds(start, 256)
        table = dequantized(codes_ref[part, :], scales_ref[part, :], spread)
        table_ref[part, :] = table.astype(BF)


def fetch_kernel(asked_ref, table_ref, out_ref):
    senders, cap = asked_ref.shape
    stride = table_ref.shape[0] // cap
    asked = asked_ref[...].astype(F32).astype(BF)
    part, width = 8 * senders, 8 * stride
    pick = (iota((part, senders), 0) // 8 == iota((part, senders), 1)).astype(F32).astype(BF)
    lists = jnp.dot(pick, asked, preferred_element_type=F32)
    entry = iota((part, 1), 0) % 8
    halves = []
    for at in range(cap // 8):
        own = iota((part, cap), 1) == iota((part, cap), 0) % 8 + at * 8
        offset = jnp.sum(jnp.where(own, lists, 0.0), axis=1, keepdims=True).astype(jnp.int32)
        target = jnp.where(offset >= 0, entry * stride + offset, -1)
        chosen = (iota((part, width), 1) == target).astype(F32).astype(BF)
        got = jnp.dot(chosen, table_ref[pl.ds(at * width, width), :], preferred_element_type=F32)
        halves.append(got.reshape(senders, 8, C))
        if at % 2 == 1:
            both = jnp.concatenate(halves, axis=1)
            out_ref[:, pl.ds((at - 1) * 8, 16), :] = both.astype(BF)
            halves = []


def sigmoid(values):
    return 0.5 + 0.5 * jnp.tanh(0.5 * values)


def train_kernel(
    place_ref,
    slots_ref,
    code_ref,
    fetched_ref,
    gain_ref,
    upstream_ref,
    *refs,
):
    weight_refs, refs = refs[: LAYERS * TAPS], refs[LAYERS * TAPS :]
    slot_grad_ref, keep_ref, send_ref, held_ref, conv_ref, unit_ref = refs[:6]
    scale_ref, grad_ref, wide_ref, weight_grad_ref = refs[6:]
    split, x, y, core = place_ref[0], place_ref[1], place_ref[2], place_ref[3]
    steps = range(0, PACKED, STEP)
    line = iota((PACKED, C), 0)
    since = jnp.where(line >= split, line - split, line)
    until = jnp.where(line >= split, PACKED - line, split - line)

    source = iota((PACKED, 1), 0)
    source = jnp.where(source >= split, source + (LEN - split), source)
    match = iota((PACKED, 2 * LEN), 1) == source
    packer = match.astype(F32).astype(BF)
    slot = jnp.where(match, slots_ref[...].astype(F32), 0.0)
    slot = jnp.sum(slot, axis=1, keepdims=True).astype(jnp.int32)
    slots = fetched_ref.shape[0]
    chosen = (iota((PACKED, slots), 1) == slot).astype(F32).astype(BF)
    first = jnp.dot(chosen, fetched_ref[...], preferred_element_type=F32)
    held_ref[0] = first.astype(BF)

    for layer in range(LAYERS):
        gap = DILATIONS[layer]
        now = held_ref[layer].astype(F32)
        taps = [held_ref[layer]]
        for tap in (1, 2):
            moved = pltpu.roll(now, tap * gap, 0)
            taps.append(jnp.where(since >= tap * gap, moved, 0.0).astype(BF))
        conv_ref[...] = jnp.dot(
            jnp.concatenate(taps, axis=1),
            jnp.concatenate([ref[...] for ref in weight_refs[layer * TAPS :][:TAPS]], axis=0),
            preferred_element_type=F32,
        )
        gain = gain_ref[pl.ds(layer, 1), :]
        for start in steps:
            part = pl.ds(start, STEP)
            value = conv_ref[part, :]
            center = value - jnp.mean(value, axis=1, keepdims=True)
            spread = jnp.mean(center * center, axis=1, keepdims=True)
            scale = lax.rsqrt(spread + 1e-5)
            unit = center * scale
            unit_ref[layer, part, :] = unit
            scale_ref[layer, part, :] = jnp.broadcast_to(scale, (STEP, 128))
            if layer + 1 < LAYERS:
                gained = unit * gain
                after = gained * sigmoid(gained)
                if layer % 2 == 1:
                    after = after + held_ref[layer - 1, part, :].astype(F32)
                held_ref[layer + 1, part, :] = after.astype(BF)

    upstream = jnp.dot(packer, upstream_ref[...], preferred_element_type=F32)
    grad_ref[...] = upstream
    held_ref[5] = upstream.astype(BF)

    gain_rows = [None] * LAYERS
    for layer in reversed(range(LAYERS)):
        gap = DILATIONS[layer]
        gain = gain_ref[pl.ds(layer, 1), :]
        total = jnp.zeros((8, C), F32)
        for start in steps:
            part = pl.ds(start, STEP)
            unit = unit_ref[layer, part, :]
            scale = scale_ref[layer, part, :]
            gained = unit * gain
            gate = sigmoid(gained)
            inner = grad_ref[part, :] * (gate * (1.0 + gained * (1.0 - gate)))
            total = total + jnp.sum((inner * unit).reshape(STEP // 8, 8, C), axis=0)
            inner = inner * gain
            mean = jnp.mean(inner, axis=1, keepdims=True)
            slope = jnp.mean(inner * unit, axis=1, keepdims=True)
            outer = inner - mean - unit * slope
            conv_ref[part, :] = outer * jnp.concatenate([scale, scale], axis=1)
        gain_rows[layer] = jnp.sum(total, axis=0, keepdims=True)
        now = conv_ref[...]
        wide_ref[:, 0:C] = now.astype(BF)
        for tap in (1, 2):
            moved = pltpu.roll(now, PACKED - tap * gap, 0)
            moved = jnp.where(until > tap * gap, moved, 0.0)
            wide_ref[:, tap * C : (tap + 1) * C] = moved.astype(BF)

        below = jnp.zeros((PACKED, C), F32)
        for tap in range(TAPS):
            kernel = weight_refs[layer * TAPS + tap][...]
            below = below + lax.dot_general(
                wide_ref[:, tap * C : (tap + 1) * C], kernel, NT, preferred_element_type=F32
            )
        if layer % 2 == 0:
            if layer == 2:
                skip = held_ref[5].astype(F32)
            else:
                skip = held_ref[4].astype(F32)
            below = below + skip
        rounded = below.astype(BF)
        grad_ref[...] = rounded.astype(F32)
        if layer == 2:
            held_ref[4] = rounded

        weight_grad = lax.dot_general(
            held_ref[layer], wide_ref[...], TN, preferred_element_type=F32
        )
        for tap in range(TAPS):
            weight_grad_ref[pl.ds(tap * C, C), :] = weight_grad[:, tap * C : (tap + 1) * C]

        for pair in range(4):
            even = weight_grad_ref[pl.ds(2 * pair * PIECE, PIECE), :]
            odd = weight_grad_ref[pl.ds((2 * pair + 1) * PIECE, PIECE), :]
            tail = jnp.zeros((TAIL, C), F32)
            even_tail = tail
            if layer == 0 and pair == 0:
                exact = jnp.concatenate(gain_rows + gain_rows, axis=0)
                high = exact.astype(BF).astype(F32)
                even_tail = jnp.where(iota((TAIL, C), 0) < LAYERS, high, exact - high)
            even = jnp.concatenate([even, even_tail], axis=0)
            odd = jnp.concatenate([odd, tail], axis=0)
            place = ((pair - y + 4) % 4) * 4 + (layer - x + 4) % 4
            keep_ref[place] = jnp.where(core == 0, even, odd).astype(BF)
            send_ref[place] = jnp.where(core == 0, odd, even).astype(BF)

    mine = grad_ref[...].astype(BF)
    for start in range(0, slots, 256):
        here = iota((256, PACKED), 0) + start == code_ref[...]
        here = here.astype(F32).astype(BF)
        summed = jnp.dot(here, mine, preferred_element_type=F32)
        slot_grad_ref[pl.ds(start, 256), :] = summed.astype(BF)


def settle(total):
    tail = total[PIECE:SLAB, :]
    exact = tail + pltpu.roll(tail, LAYERS, 0)
    high = exact.astype(BF).astype(F32)
    tail = jnp.where(iota((TAIL, C), 0) < LAYERS, high, exact - high)
    return jnp.concatenate([total[:PIECE, :], tail], axis=0).astype(BF)


def core_sum_kernel(keep_ref, got_ref, *out_refs):
    for at in range(16):
        total = keep_ref[at].astype(F32) + got_ref[at].astype(F32)
        out_refs[at // 4][at % 4] = settle(total)


def four_sum_kernel(a_ref, b_ref, c_ref, d_ref, *out_refs):
    for at in range(a_ref.shape[0]):
        left = a_ref[at].astype(F32) + b_ref[at].astype(F32)
        right = c_ref[at].astype(F32) + d_ref[at].astype(F32)
        out_refs[at][0] = settle(left + right)


def last_sum_kernel(a_ref, b_ref, *refs):
    slab = settle(a_ref[0].astype(F32) + b_ref[0].astype(F32)).astype(F32)
    rows = refs[0][0].astype(F32) + refs[1][0].astype(F32)
    refs[2][...] = jnp.concatenate([rows, slab], axis=0).astype(BF)


def part_kernel(*refs):
    for at, ref in zip((0, 1, 3, 2), refs[:4]):
        both = ref[...].astype(F32)
        refs[4][at] = both[:C].astype(BF)
        refs[5][at] = both[C:].astype(BF)


def spread_kernel(count, plan, first, place_ref, *refs):
    sources, refs = refs[:count], refs[count:]
    if not first:
        gain_before, refs = refs[1], refs[2:]
    conv_hbm, gain_ref, wide_ref, sems = refs
    x, y, core = place_ref[1], place_ref[2], place_ref[3]
    gain_ref[...] = jnp.zeros_like(gain_ref) if first else gain_before[...]
    leaving = []
    for at, (buffer, inner, along_x, along_y, other) in enumerate(plan):
        layer = (x + along_x) % 4
        side = core if other == 0 else 1 - core
        number = layer * 8 + ((y + along_y) % 4) * 2 + side
        block = sources[buffer][inner].astype(F32)
        wide_ref[at] = block[:PIECE, :]
        copy = pltpu.make_async_copy(
            wide_ref.at[at],
            conv_hbm.at[pl.ds(pl.multiple_of(number * PIECE, PIECE), PIECE)],
            sems.at[at],
        )
        copy.start()
        leaving.append(copy)

        @pl.when(number == 0)
        def _():
            tail = block[PIECE:, :]
            gain_ref[...] = (tail + pltpu.roll(tail, LAYERS, 0))[:LAYERS, :]

    for copy in leaving:
        copy.wait()


def spread(place, blocks, plan, before=None):
    outs = [shape((LAYERS * TAPS * C, C), F32), shape((LAYERS, C), F32)]
    count = len(blocks)
    args, specs, aliases = [place] + blocks, [SMEM] + [VMEM] * count, {}
    if before is not None:
        args, specs = args + list(before), specs + [HBM, VMEM]
        aliases = {count + 1: 0}
    return pl.pallas_call(
        functools.partial(spread_kernel, count, plan, before is None),
        out_shape=outs,
        in_specs=specs,
        out_specs=[HBM, VMEM],
        input_output_aliases=aliases,
        scratch_shapes=[
            pltpu.VMEM((len(plan), PIECE, C), F32),
            pltpu.SemaphoreType.DMA((len(plan),)),
        ],
        compiler_params=pltpu.CompilerParams(vmem_limit_bytes=8 * 1024 * 1024),
        cost_estimate=pl.CostEstimate(flops=0, bytes_accessed=1 << 21, transcendentals=0),
    )(*args)


def scatter_kernel(place_ref, code_ref, got_ref, keep_ref, send_ref):
    y, core = place_ref[2], place_ref[3]
    senders = got_ref.shape[0]
    lines = code_ref.shape[1]
    for pair in range(4):
        if pair % 2 == 0:
            both = got_ref[:, pl.ds(pair * 8, 16), :].astype(F32).reshape(senders, 2, 8, C)
        got = both[:, pair % 2].reshape(lines, C).astype(BF)
        here = iota((2 * C, lines), 0) + pair * 2 * C == code_ref[pl.ds(pair, 1), :]
        here = here.astype(F32).astype(BF)
        total = jnp.dot(here, got, preferred_element_type=F32)
        even, odd = total[:C], total[C:]
        apart = pair ^ y
        place = jnp.where(apart == 3, 1, jnp.where(apart == 0, 0, apart + 1))
        keep_ref[place] = jnp.where(core == 0, even, odd).astype(BF)
        send_ref[place] = jnp.where(core == 0, odd, even).astype(BF)


def row_sum_kernel(keep_ref, got_ref, *out_refs):
    half = keep_ref.shape[0] // 2
    total = (keep_ref[...].astype(F32) + got_ref[...].astype(F32)).astype(BF)
    out_refs[0][...] = total[:half]
    out_refs[1][...] = total[half:]


def adagrad_kernel(place_ref, *refs):
    own_ref, across_ref, codes_ref, scales_ref, accum_ref = refs[:5]
    rows_hbm, next_ref, rows_ref, sems = refs[5:]
    spread = spreader(scales_ref.shape[1])
    y, core = place_ref[2], place_ref[3]
    same = iota((C, C), 0) == iota((C, C), 1)
    half = C // 2
    leaving = []
    for at in range(8):
        side = core if at < 4 else 1 - core
        number = ((y + at % 4) % 4) * 2 + side
        part = pl.ds(pl.multiple_of(number * C, C), C)
        gradient = (own_ref[at] if at < 4 else across_ref[at - 4]).astype(F32)
        lines = [accum_ref[pl.ds(2 * number + side, 1), :] for side in range(2)]
        line = jnp.concatenate(lines, axis=1)
        grown = jnp.sum(jnp.where(same, line, 0.0), axis=1, keepdims=True)
        grown = grown + jnp.mean(gradient * gradient, axis=1, keepdims=True)
        table = dequantized(codes_ref[part, :], scales_ref[part, :], spread)
        rows_ref[at] = table - LEARN_RATE * gradient * lax.rsqrt(grown)
        copy = pltpu.make_async_copy(rows_ref.at[at], rows_hbm.at[part], sems.at[at])
        copy.start()
        leaving.append(copy)
        line = jnp.sum(jnp.where(same, grown, 0.0), axis=0, keepdims=True)
        next_ref[pl.ds(2 * number, 1), :] = line[:, :half]
        next_ref[pl.ds(2 * number + 1, 1), :] = line[:, half:]
    for copy in leaving:
        copy.wait()


def shifted(values, axis, size, offset):
    return lax.ppermute(values, axis, [(i, (i + offset) % size) for i in range(size)])


def crossed(values, axis, size, bits):
    return lax.ppermute(values, axis, [(i, i ^ bits) for i in range(size)])


def after(values, *others):
    return lax.optimization_barrier((values, *others))[0]


def body(lengths, slots, requests, counts, codes, scales, accum, conv_weight, norm_gain, upstream):
    table_axes = ("x", "z")
    owners = requests.shape[1]
    cap = requests.shape[2]
    rows = codes.shape[0]
    stride = rows // cap
    split = lengths[0, 0]
    place = jnp.stack(
        [split, lax.axis_index("x"), lax.axis_index("y"), lax.axis_index("core")]
    ).astype(jnp.int32)

    entry = jnp.arange(cap, dtype=jnp.int32)[None, :]
    wanted = jnp.where(entry < counts[0][:, None], requests[0] - entry * stride, -1)
    asked = lax.all_to_all(wanted, table_axes, split_axis=0, concat_axis=0, tiled=True)

    order = jnp.arange(PACKED, dtype=jnp.int32)
    order = order + jnp.where(order >= split, LEN - split, 0)
    match = order[:, None] == jnp.arange(2 * LEN, dtype=jnp.int32)[None, :]
    packed = jnp.sum(jnp.where(match, slots.reshape(1, 2 * LEN), 0), axis=1)

    table = call(table_kernel, shape((rows, C), BF), [codes, scales], flops=1 << 24)
    sending = call(
        fetch_kernel, shape((owners, cap, C), BF), [asked, table], flops=1 << 30
    )
    fetched = lax.all_to_all(
        sending, table_axes, split_axis=0, concat_axis=0, tiled=True
    ).reshape(owners * cap, C)

    target = jnp.where(asked >= 0, asked + entry * stride, -1)
    target = target.reshape(owners, 4, 8).transpose(1, 0, 2).reshape(4, 8 * owners)
    fetched, target = lax.optimization_barrier((fetched, target))

    slab16 = shape((16, SLAB, C), BF)
    slot_grad, keep, send = call(
        train_kernel,
        [shape((owners * cap, C), BF), slab16, slab16],
        [
            place,
            slots.reshape(1, 2 * LEN),
            packed.reshape(1, PACKED),
            fetched,
            norm_gain,
            upstream.reshape(2 * LEN, C),
            *[conv_weight[layer, tap] for layer in range(LAYERS) for tap in range(TAPS)],
        ],
        specs=[SMEM] + [VMEM] * 17,
        scratch=[
            pltpu.VMEM((LAYERS + 2, PACKED, C), BF),
            pltpu.VMEM((PACKED, C), F32),
            pltpu.VMEM((LAYERS, PACKED, C), F32),
            pltpu.VMEM((LAYERS, PACKED, 128), F32),
            pltpu.VMEM((PACKED, C), F32),
            pltpu.VMEM((PACKED, TAPS * C), BF),
            pltpu.VMEM((TAPS * C, C), F32),
        ],
        flops=1 << 32,
        limit=16,
    )

    got = crossed(send, "core", 2, 1)
    returned = lax.all_to_all(
        slot_grad.reshape(owners, cap, C), table_axes, split_axis=0, concat_axis=0, tiled=True
    )
    slab4, slab1 = shape((4, SLAB, C), BF), shape((1, SLAB, C), BF)
    block4 = shape((4, C, C), BF)

    parts = call(core_sum_kernel, [slab4] * 4, [keep, got])
    parts = [parts[0]] + [shifted(parts[k], "y", 4, k) for k in (2, 1, 3)]
    parts = call(four_sum_kernel, [slab1] * 4, parts)
    keep_rows, send_rows = call(
        scatter_kernel,
        [block4, block4],
        [place, target, after(returned, parts[0])],
        specs=[SMEM, VMEM, VMEM],
        flops=1 << 29,
    )
    parts = [parts[0]] + [shifted(parts[k], "x", 4, k) for k in (2, 1, 3)]
    sums = [keep_rows, crossed(send_rows, "core", 2, 1)]
    parts, sums = lax.optimization_barrier((parts, sums))

    (part,) = call(four_sum_kernel, [slab1], parts)
    keep_rows, send_rows = call(row_sum_kernel, [shape((2, C, C), BF)] * 2, sums)
    parts = [part] + [crossed(part, "z", 8, k) for k in (1, 2, 3)]
    sums = [keep_rows, crossed(send_rows, "y", 4, 1)]
    parts, sums = lax.optimization_barrier((parts, sums))
    (part,) = call(four_sum_kernel, [slab1], parts)
    keep_rows, send_rows = call(row_sum_kernel, [shape((1, C, C), BF)] * 2, sums)
    parts = [part, crossed(part, "z", 8, 6)]
    sums = [keep_rows, crossed(send_rows, "y", 4, 3)]
    parts, sums = lax.optimization_barrier((parts, sums))

    part = call(last_sum_kernel, shape((C + SLAB, C), BF), parts + sums)
    parts = [part] + [shifted(part, "y", 4, -k) for k in (1, 3, 2)]
    mine, parts = call(part_kernel, [block4, slab4], parts)
    later = [shifted(parts, "x", 4, -k) for k in (1, 3, 2)]
    across = crossed(mine, "core", 2, 1)
    new_rows, next_accum = call(
        adagrad_kernel,
        [shape((rows, C), F32), shape((rows // 128, 128), F32)],
        [place, mine, across, codes, scales, accum.reshape(rows // 128, 128)],
        specs=[SMEM] + [VMEM] * 5,
        out_specs=[HBM, VMEM],
        scratch=[pltpu.VMEM((8, C, C), F32), pltpu.SemaphoreType.DMA((8,))],
    )
    later = after(later, next_accum)
    held = [parts] + later
    order = (0, 1, 3, 2)
    plan = [(at, inner, order[at], inner, 0) for at in range(4) for inner in range(4)]
    filled = spread(place, held, plan)
    plan = [(at, inner, order[at], inner, 1) for at in range(4) for inner in range(4)]
    beyond = [crossed(part, "core", 2, 1) for part in held]
    grad_conv, grad_gain = spread(place, beyond, plan, filled)
    return (
        new_rows,
        next_accum.reshape(rows),
        grad_conv.reshape(conv_weight.shape),
        grad_gain,
    )


def solution(mesh):
    fine = Mesh(mesh.devices.reshape(4, 8, 4, 2), ("x", "z", "y", "core"))
    every = ("x", "z", "y", "core")
    table = ("x", "z")
    return jax.shard_map(
        body,
        mesh=fine,
        in_specs=(
            P(every, None),
            P(every, None),
            P(every, None, None),
            P(every, None),
            P(table, None),
            P(table, None),
            P(table),
            P(),
            P(),
            P(every, None, None),
        ),
        out_specs=(P(table, None), P(table), P(), P()),
        check_vma=False,
    )
```

```python
import functools

import jax
import jax.numpy as jnp
from jax import lax
from jax.experimental import pallas as pl
from jax.experimental.pallas import tpu as pltpu
from jax.sharding import Mesh
from jax.sharding import PartitionSpec as P

DILATIONS = (1, 2, 4, 8)
LEARN_RATE = 0.5
BF = jnp.bfloat16
F32 = jnp.float32
LAYERS, TAPS, C = 4, 3, 256
GROUP = 32
LEN = 256
PACKED = 320
STEP = 64
PIECE = 96
TAIL = 8
SLAB = PIECE + TAIL
NT = (((1,), (1,)), ((), ()))
TN = (((0,), (0,)), ((), ()))
SMEM = pl.BlockSpec(memory_space=pltpu.SMEM)
VMEM = pl.BlockSpec(memory_space=pltpu.VMEM)
ANY = pl.BlockSpec(memory_space=pl.ANY)
HBM = pl.BlockSpec(memory_space=pltpu.HBM)


def call(kernel, outs, args, specs=None, out_specs=None, scratch=(), flops=0, limit=8):
    if specs is None:
        specs = [VMEM] * len(args)
    if out_specs is None:
        out_specs = jax.tree.map(lambda _: VMEM, outs)
    return pl.pallas_call(
        kernel,
        out_shape=outs,
        in_specs=specs,
        out_specs=out_specs,
        scratch_shapes=list(scratch),
        compiler_params=pltpu.CompilerParams(vmem_limit_bytes=limit * 1024 * 1024),
        cost_estimate=pl.CostEstimate(flops=flops, bytes_accessed=1 << 20, transcendentals=0),
    )(*args)


def shape(dims, dtype):
    return jax.ShapeDtypeStruct(dims, dtype)


def iota(dims, axis):
    return lax.broadcasted_iota(jnp.int32, dims, axis)


def spreader(groups):
    return (iota((groups, C), 1) // GROUP == iota((groups, C), 0)).astype(F32).astype(BF)


def dequantized(codes, scales, spread):
    return codes.astype(F32) * jnp.dot(scales, spread, preferred_element_type=F32)


def table_kernel(codes_ref, scales_ref, table_ref):
    spread = spreader(scales_ref.shape[1])
    for start in range(0, codes_ref.shape[0], 256):
        part = pl.ds(start, 256)
        table = dequantized(codes_ref[part, :], scales_ref[part, :], spread)
        table_ref[part, :] = table.astype(BF)


def fetch_kernel(asked_ref, table_ref, out_ref):
    senders, cap = asked_ref.shape
    stride = table_ref.shape[0] // cap
    asked = asked_ref[...].astype(F32).astype(BF)
    part, width = 8 * senders, 8 * stride
    pick = (iota((part, senders), 0) // 8 == iota((part, senders), 1)).astype(F32).astype(BF)
    lists = jnp.dot(pick, asked, preferred_element_type=F32)
    entry = iota((part, 1), 0) % 8
    halves = []
    for at in range(cap // 8):
        own = iota((part, cap), 1) == iota((part, cap), 0) % 8 + at * 8
        offset = jnp.sum(jnp.where(own, lists, 0.0), axis=1, keepdims=True).astype(jnp.int32)
        target = jnp.where(offset >= 0, entry * stride + offset, -1)
        chosen = (iota((part, width), 1) == target).astype(F32).astype(BF)
        got = jnp.dot(chosen, table_ref[pl.ds(at * width, width), :], preferred_element_type=F32)
        halves.append(got.reshape(senders, 8, C))
        if at % 2 == 1:
            both = jnp.concatenate(halves, axis=1)
            out_ref[:, pl.ds((at - 1) * 8, 16), :] = both.astype(BF)
            halves = []


def sigmoid(values):
    return 0.5 + 0.5 * jnp.tanh(0.5 * values)


def train_kernel(
    place_ref,
    slots_ref,
    code_ref,
    fetched_ref,
    gain_ref,
    upstream_ref,
    *refs,
):
    weight_refs, refs = refs[: LAYERS * TAPS], refs[LAYERS * TAPS :]
    slot_grad_ref, keep_ref, send_ref, held_ref, conv_ref, unit_ref = refs[:6]
    scale_ref, grad_ref, wide_ref, weight_grad_ref = refs[6:]
    split, x, y, core = place_ref[0], place_ref[1], place_ref[2], place_ref[3]
    steps = range(0, PACKED, STEP)
    line = iota((PACKED, C), 0)
    since = jnp.where(line >= split, line - split, line)
    until = jnp.where(line >= split, PACKED - line, split - line)

    source = iota((PACKED, 1), 0)
    source = jnp.where(source >= split, source + (LEN - split), source)
    match = iota((PACKED, 2 * LEN), 1) == source
    packer = match.astype(F32).astype(BF)
    slot = jnp.where(match, slots_ref[...].astype(F32), 0.0)
    slot = jnp.sum(slot, axis=1, keepdims=True).astype(jnp.int32)
    slots = fetched_ref.shape[0]
    chosen = (iota((PACKED, slots), 1) == slot).astype(F32).astype(BF)
    first = jnp.dot(chosen, fetched_ref[...], preferred_element_type=F32)
    held_ref[0] = first.astype(BF)

    for layer in range(LAYERS):
        gap = DILATIONS[layer]
        now = held_ref[layer].astype(F32)
        taps = [held_ref[layer]]
        for tap in (1, 2):
            moved = pltpu.roll(now, tap * gap, 0)
            taps.append(jnp.where(since >= tap * gap, moved, 0.0).astype(BF))
        conv_ref[...] = jnp.dot(
            jnp.concatenate(taps, axis=1),
            jnp.concatenate([ref[...] for ref in weight_refs[layer * TAPS :][:TAPS]], axis=0),
            preferred_element_type=F32,
        )
        gain = gain_ref[pl.ds(layer, 1), :]
        for start in steps:
            part = pl.ds(start, STEP)
            value = conv_ref[part, :]
            center = value - jnp.mean(value, axis=1, keepdims=True)
            spread = jnp.mean(center * center, axis=1, keepdims=True)
            scale = lax.rsqrt(spread + 1e-5)
            unit = center * scale
            unit_ref[layer, part, :] = unit
            scale_ref[layer, part, :] = jnp.broadcast_to(scale, (STEP, 128))
            if layer + 1 < LAYERS:
                gained = unit * gain
                after = gained * sigmoid(gained)
                if layer % 2 == 1:
                    after = after + held_ref[layer - 1, part, :].astype(F32)
                held_ref[layer + 1, part, :] = after.astype(BF)

    upstream = jnp.dot(packer, upstream_ref[...], preferred_element_type=F32)
    grad_ref[...] = upstream
    held_ref[5] = upstream.astype(BF)

    gain_rows = [None] * LAYERS
    for layer in reversed(range(LAYERS)):
        gap = DILATIONS[layer]
        gain = gain_ref[pl.ds(layer, 1), :]
        total = jnp.zeros((8, C), F32)
        for start in steps:
            part = pl.ds(start, STEP)
            unit = unit_ref[layer, part, :]
            scale = scale_ref[layer, part, :]
            gained = unit * gain
            gate = sigmoid(gained)
            inner = grad_ref[part, :] * (gate * (1.0 + gained * (1.0 - gate)))
            total = total + jnp.sum((inner * unit).reshape(STEP // 8, 8, C), axis=0)
            inner = inner * gain
            mean = jnp.mean(inner, axis=1, keepdims=True)
            slope = jnp.mean(inner * unit, axis=1, keepdims=True)
            outer = inner - mean - unit * slope
            conv_ref[part, :] = outer * jnp.concatenate([scale, scale], axis=1)
        gain_rows[layer] = jnp.sum(total, axis=0, keepdims=True)
        now = conv_ref[...]
        wide_ref[:, 0:C] = now.astype(BF)
        for tap in (1, 2):
            moved = pltpu.roll(now, PACKED - tap * gap, 0)
            moved = jnp.where(until > tap * gap, moved, 0.0)
            wide_ref[:, tap * C : (tap + 1) * C] = moved.astype(BF)

        below = jnp.zeros((PACKED, C), F32)
        for tap in range(TAPS):
            kernel = weight_refs[layer * TAPS + tap][...]
            below = below + lax.dot_general(
                wide_ref[:, tap * C : (tap + 1) * C], kernel, NT, preferred_element_type=F32
            )
        if layer % 2 == 0:
            if layer == 2:
                skip = held_ref[5].astype(F32)
            else:
                skip = held_ref[4].astype(F32)
            below = below + skip
        rounded = below.astype(BF)
        grad_ref[...] = rounded.astype(F32)
        if layer == 2:
            held_ref[4] = rounded

        weight_grad = lax.dot_general(
            held_ref[layer], wide_ref[...], TN, preferred_element_type=F32
        )
        for tap in range(TAPS):
            weight_grad_ref[pl.ds(tap * C, C), :] = weight_grad[:, tap * C : (tap + 1) * C]

        for pair in range(4):
            even = weight_grad_ref[pl.ds(2 * pair * PIECE, PIECE), :]
            odd = weight_grad_ref[pl.ds((2 * pair + 1) * PIECE, PIECE), :]
            tail = jnp.zeros((TAIL, C), F32)
            even_tail = tail
            if layer == 0 and pair == 0:
                exact = jnp.concatenate(gain_rows + gain_rows, axis=0)
                high = exact.astype(BF).astype(F32)
                even_tail = jnp.where(iota((TAIL, C), 0) < LAYERS, high, exact - high)
            even = jnp.concatenate([even, even_tail], axis=0)
            odd = jnp.concatenate([odd, tail], axis=0)
            place = ((pair - y + 4) % 4) * 4 + (layer - x + 4) % 4
            keep_ref[place] = jnp.where(core == 0, even, odd).astype(BF)
            send_ref[place] = jnp.where(core == 0, odd, even).astype(BF)

    mine = grad_ref[...].astype(BF)
    for start in range(0, slots, 256):
        here = iota((256, PACKED), 0) + start == code_ref[...]
        here = here.astype(F32).astype(BF)
        summed = jnp.dot(here, mine, preferred_element_type=F32)
        slot_grad_ref[pl.ds(start, 256), :] = summed.astype(BF)


def settle(total):
    tail = total[PIECE:SLAB, :]
    exact = tail + pltpu.roll(tail, LAYERS, 0)
    high = exact.astype(BF).astype(F32)
    tail = jnp.where(iota((TAIL, C), 0) < LAYERS, high, exact - high)
    return jnp.concatenate([total[:PIECE, :], tail], axis=0).astype(BF)


def core_sum_kernel(keep_ref, got_ref, *out_refs):
    for at in range(16):
        total = keep_ref[at].astype(F32) + got_ref[at].astype(F32)
        out_refs[at // 4][at % 4] = settle(total)


def four_sum_kernel(a_ref, b_ref, c_ref, d_ref, *out_refs):
    for at in range(a_ref.shape[0]):
        left = a_ref[at].astype(F32) + b_ref[at].astype(F32)
        right = c_ref[at].astype(F32) + d_ref[at].astype(F32)
        out_refs[at][0] = settle(left + right)


def last_sum_kernel(a_ref, b_ref, *refs):
    slab = settle(a_ref[0].astype(F32) + b_ref[0].astype(F32)).astype(F32)
    rows = refs[0][0].astype(F32) + refs[1][0].astype(F32)
    refs[2][...] = jnp.concatenate([rows, slab], axis=0).astype(BF)


def part_kernel(*refs):
    for at, ref in zip((0, 1, 3, 2), refs[:4]):
        both = ref[...].astype(F32)
        refs[4][at] = both[:C].astype(BF)
        refs[5][at] = both[C:].astype(BF)


def spread_kernel(count, plan, first, place_ref, *refs):
    sources, refs = refs[:count], refs[count:]
    if not first:
        gain_before, refs = refs[1], refs[2:]
    conv_hbm, gain_ref, wide_ref, sems = refs
    x, y, core = place_ref[1], place_ref[2], place_ref[3]
    gain_ref[...] = jnp.zeros_like(gain_ref) if first else gain_before[...]
    leaving = []
    for at, (buffer, inner, along_x, along_y, other) in enumerate(plan):
        layer = (x + along_x) % 4
        side = core if other == 0 else 1 - core
        number = layer * 8 + ((y + along_y) % 4) * 2 + side
        block = sources[buffer][inner].astype(F32)
        wide_ref[at] = block[:PIECE, :]
        copy = pltpu.make_async_copy(
            wide_ref.at[at],
            conv_hbm.at[pl.ds(pl.multiple_of(number * PIECE, PIECE), PIECE)],
            sems.at[at],
        )
        copy.start()
        leaving.append(copy)

        @pl.when(number == 0)
        def _():
            tail = block[PIECE:, :]
            gain_ref[...] = (tail + pltpu.roll(tail, LAYERS, 0))[:LAYERS, :]

    for copy in leaving:
        copy.wait()


def spread(place, blocks, plan, before=None):
    outs = [shape((LAYERS * TAPS * C, C), F32), shape((LAYERS, C), F32)]
    count = len(blocks)
    args, specs, aliases = [place] + blocks, [SMEM] + [VMEM] * count, {}
    if before is not None:
        args, specs = args + list(before), specs + [HBM, VMEM]
        aliases = {count + 1: 0}
    return pl.pallas_call(
        functools.partial(spread_kernel, count, plan, before is None),
        out_shape=outs,
        in_specs=specs,
        out_specs=[HBM, VMEM],
        input_output_aliases=aliases,
        scratch_shapes=[
            pltpu.VMEM((len(plan), PIECE, C), F32),
            pltpu.SemaphoreType.DMA((len(plan),)),
        ],
        compiler_params=pltpu.CompilerParams(vmem_limit_bytes=8 * 1024 * 1024),
        cost_estimate=pl.CostEstimate(flops=0, bytes_accessed=1 << 21, transcendentals=0),
    )(*args)


def scatter_kernel(place_ref, code_ref, got_ref, keep_ref, send_ref):
    y, core = place_ref[2], place_ref[3]
    senders = got_ref.shape[0]
    lines = code_ref.shape[1]
    for pair in range(4):
        if pair % 2 == 0:
            both = got_ref[:, pl.ds(pair * 8, 16), :].astype(F32).reshape(senders, 2, 8, C)
        got = both[:, pair % 2].reshape(lines, C).astype(BF)
        here = iota((2 * C, lines), 0) + pair * 2 * C == code_ref[pl.ds(pair, 1), :]
        here = here.astype(F32).astype(BF)
        total = jnp.dot(here, got, preferred_element_type=F32)
        even, odd = total[:C], total[C:]
        apart = pair ^ y
        place = jnp.where(apart == 3, 1, jnp.where(apart == 0, 0, apart + 1))
        keep_ref[place] = jnp.where(core == 0, even, odd).astype(BF)
        send_ref[place] = jnp.where(core == 0, odd, even).astype(BF)


def row_sum_kernel(keep_ref, got_ref, *out_refs):
    half = keep_ref.shape[0] // 2
    total = (keep_ref[...].astype(F32) + got_ref[...].astype(F32)).astype(BF)
    out_refs[0][...] = total[:half]
    out_refs[1][...] = total[half:]


def adagrad_kernel(place_ref, *refs):
    own_ref, across_ref, codes_ref, scales_ref, accum_ref = refs[:5]
    rows_hbm, next_ref, rows_ref, sems = refs[5:]
    spread = spreader(scales_ref.shape[1])
    y, core = place_ref[2], place_ref[3]
    same = iota((C, C), 0) == iota((C, C), 1)
    half = C // 2
    leaving = []
    for at in range(8):
        side = core if at < 4 else 1 - core
        number = ((y + at % 4) % 4) * 2 + side
        part = pl.ds(pl.multiple_of(number * C, C), C)
        gradient = (own_ref[at] if at < 4 else across_ref[at - 4]).astype(F32)
        lines = [accum_ref[pl.ds(2 * number + side, 1), :] for side in range(2)]
        line = jnp.concatenate(lines, axis=1)
        grown = jnp.sum(jnp.where(same, line, 0.0), axis=1, keepdims=True)
        grown = grown + jnp.mean(gradient * gradient, axis=1, keepdims=True)
        table = dequantized(codes_ref[part, :], scales_ref[part, :], spread)
        rows_ref[at] = table - LEARN_RATE * gradient * lax.rsqrt(grown)
        copy = pltpu.make_async_copy(rows_ref.at[at], rows_hbm.at[part], sems.at[at])
        copy.start()
        leaving.append(copy)
        line = jnp.sum(jnp.where(same, grown, 0.0), axis=0, keepdims=True)
        next_ref[pl.ds(2 * number, 1), :] = line[:, :half]
        next_ref[pl.ds(2 * number + 1, 1), :] = line[:, half:]
    for copy in leaving:
        copy.wait()


def shifted(values, axis, size, offset):
    return lax.ppermute(values, axis, [(i, (i + offset) % size) for i in range(size)])


def crossed(values, axis, size, bits):
    return lax.ppermute(values, axis, [(i, i ^ bits) for i in range(size)])


def after(values, *others):
    return lax.optimization_barrier((values, *others))[0]


def body(lengths, slots, requests, counts, codes, scales, accum, conv_weight, norm_gain, upstream):
    table_axes = ("x", "z")
    owners = requests.shape[1]
    cap = requests.shape[2]
    rows = codes.shape[0]
    stride = rows // cap
    split = lengths[0, 0]
    place = jnp.stack(
        [split, lax.axis_index("x"), lax.axis_index("y"), lax.axis_index("core")]
    ).astype(jnp.int32)

    entry = jnp.arange(cap, dtype=jnp.int32)[None, :]
    wanted = jnp.where(entry < counts[0][:, None], requests[0] - entry * stride, -1)
    asked = lax.all_to_all(wanted, table_axes, split_axis=0, concat_axis=0, tiled=True)

    order = jnp.arange(PACKED, dtype=jnp.int32)
    order = order + jnp.where(order >= split, LEN - split, 0)
    match = order[:, None] == jnp.arange(2 * LEN, dtype=jnp.int32)[None, :]
    packed = jnp.sum(jnp.where(match, slots.reshape(1, 2 * LEN), 0), axis=1)

    table = call(table_kernel, shape((rows, C), BF), [codes, scales], flops=1 << 24)
    sending = call(
        fetch_kernel, shape((owners, cap, C), BF), [asked, table], flops=1 << 30
    )
    fetched = lax.all_to_all(
        sending, table_axes, split_axis=0, concat_axis=0, tiled=True
    ).reshape(owners * cap, C)

    target = jnp.where(asked >= 0, asked + entry * stride, -1)
    target = target.reshape(owners, 4, 8).transpose(1, 0, 2).reshape(4, 8 * owners)
    fetched, target = lax.optimization_barrier((fetched, target))

    slab16 = shape((16, SLAB, C), BF)
    slot_grad, keep, send = call(
        train_kernel,
        [shape((owners * cap, C), BF), slab16, slab16],
        [
            place,
            slots.reshape(1, 2 * LEN),
            packed.reshape(1, PACKED),
            fetched,
            norm_gain,
            upstream.reshape(2 * LEN, C),
            *[conv_weight[layer, tap] for layer in range(LAYERS) for tap in range(TAPS)],
        ],
        specs=[SMEM] + [VMEM] * 17,
        scratch=[
            pltpu.VMEM((LAYERS + 2, PACKED, C), BF),
            pltpu.VMEM((PACKED, C), F32),
            pltpu.VMEM((LAYERS, PACKED, C), F32),
            pltpu.VMEM((LAYERS, PACKED, 128), F32),
            pltpu.VMEM((PACKED, C), F32),
            pltpu.VMEM((PACKED, TAPS * C), BF),
            pltpu.VMEM((TAPS * C, C), F32),
        ],
        flops=1 << 32,
        limit=16,
    )

    got = crossed(send, "core", 2, 1)
    returned = lax.all_to_all(
        slot_grad.reshape(owners, cap, C), table_axes, split_axis=0, concat_axis=0, tiled=True
    )
    slab4, slab1 = shape((4, SLAB, C), BF), shape((1, SLAB, C), BF)
    block4 = shape((4, C, C), BF)

    parts = call(core_sum_kernel, [slab4] * 4, [keep, got])
    parts = [parts[0]] + [shifted(parts[k], "y", 4, k) for k in (2, 1, 3)]
    parts = call(four_sum_kernel, [slab1] * 4, parts)
    keep_rows, send_rows = call(
        scatter_kernel,
        [block4, block4],
        [place, target, after(returned, parts[0])],
        specs=[SMEM, VMEM, VMEM],
        flops=1 << 29,
    )
    parts = [parts[0]] + [shifted(parts[k], "x", 4, k) for k in (2, 1, 3)]
    sums = [keep_rows, crossed(send_rows, "core", 2, 1)]
    parts, sums = lax.optimization_barrier((parts, sums))

    (part,) = call(four_sum_kernel, [slab1], parts)
    keep_rows, send_rows = call(row_sum_kernel, [shape((2, C, C), BF)] * 2, sums)
    parts = [part] + [crossed(part, "z", 8, k) for k in (1, 2, 3)]
    sums = [keep_rows, crossed(send_rows, "y", 4, 1)]
    parts, sums = lax.optimization_barrier((parts, sums))
    (part,) = call(four_sum_kernel, [slab1], parts)
    keep_rows, send_rows = call(row_sum_kernel, [shape((1, C, C), BF)] * 2, sums)
    parts = [part, crossed(part, "z", 8, 6)]
    sums = [keep_rows, crossed(send_rows, "y", 4, 3)]
    parts, sums = lax.optimization_barrier((parts, sums))

    part = call(last_sum_kernel, shape((C + SLAB, C), BF), parts + sums)
    parts = [part] + [shifted(part, "y", 4, -k) for k in (1, 3, 2)]
    mine, parts = call(part_kernel, [block4, slab4], parts)
    later = [shifted(parts, "x", 4, -k) for k in (1, 3, 2)]
    across = crossed(mine, "core", 2, 1)
    new_rows, next_accum = call(
        adagrad_kernel,
        [shape((rows, C), F32), shape((rows // 128, 128), F32)],
        [place, mine, across, codes, scales, accum.reshape(rows // 128, 128)],
        specs=[SMEM] + [VMEM] * 5,
        out_specs=[HBM, VMEM],
        scratch=[pltpu.VMEM((8, C, C), F32), pltpu.SemaphoreType.DMA((8,))],
    )
    plan = [(at, inner, 0, inner, at) for at in range(2) for inner in range(4)]
    filled = spread(place, [parts, crossed(parts, "core", 2, 1)], plan)
    later = after(later, next_accum, filled)
    order = (1, 3, 2)
    plan = [(at, inner, order[at], inner, 0) for at in range(3) for inner in range(4)]
    beyond = [crossed(part, "core", 2, 1) for part in later]
    filled = spread(place, later, plan, filled)
    plan = [(at, inner, order[at], inner, 1) for at in range(3) for inner in range(4)]
    grad_conv, grad_gain = spread(place, beyond, plan, filled)
    return (
        new_rows,
        next_accum.reshape(rows),
        grad_conv.reshape(conv_weight.shape),
        grad_gain,
    )


def solution(mesh):
    fine = Mesh(mesh.devices.reshape(4, 8, 4, 2), ("x", "z", "y", "core"))
    every = ("x", "z", "y", "core")
    table = ("x", "z")
    return jax.shard_map(
        body,
        mesh=fine,
        in_specs=(
            P(every, None),
            P(every, None),
            P(every, None, None),
            P(every, None),
            P(table, None),
            P(table, None),
            P(table),
            P(),
            P(),
            P(every, None, None),
        ),
        out_specs=(P(table, None), P(table), P(), P()),
        check_vma=False,
    )
```

```python
import functools

import jax
import jax.numpy as jnp
from jax import lax
from jax.experimental import pallas as pl
from jax.experimental.pallas import tpu as pltpu
from jax.sharding import Mesh
from jax.sharding import PartitionSpec as P

DILATIONS = (1, 2, 4, 8)
LEARN_RATE = 0.5
BF = jnp.bfloat16
F32 = jnp.float32
LAYERS, TAPS, C = 4, 3, 256
GROUP = 32
LEN = 256
PACKED = 320
STEP = 64
PIECE = 96
TAIL = 8
SLAB = PIECE + TAIL
NT = (((1,), (1,)), ((), ()))
TN = (((0,), (0,)), ((), ()))
SMEM = pl.BlockSpec(memory_space=pltpu.SMEM)
VMEM = pl.BlockSpec(memory_space=pltpu.VMEM)
ANY = pl.BlockSpec(memory_space=pl.ANY)
HBM = pl.BlockSpec(memory_space=pltpu.HBM)


def call(kernel, outs, args, specs=None, out_specs=None, scratch=(), flops=0, limit=8):
    if specs is None:
        specs = [VMEM] * len(args)
    if out_specs is None:
        out_specs = jax.tree.map(lambda _: VMEM, outs)
    return pl.pallas_call(
        kernel,
        out_shape=outs,
        in_specs=specs,
        out_specs=out_specs,
        scratch_shapes=list(scratch),
        compiler_params=pltpu.CompilerParams(vmem_limit_bytes=limit * 1024 * 1024),
        cost_estimate=pl.CostEstimate(flops=flops, bytes_accessed=1 << 20, transcendentals=0),
    )(*args)


def shape(dims, dtype):
    return jax.ShapeDtypeStruct(dims, dtype)


def iota(dims, axis):
    return lax.broadcasted_iota(jnp.int32, dims, axis)


def spreader(groups):
    return (iota((groups, C), 1) // GROUP == iota((groups, C), 0)).astype(F32).astype(BF)


def dequantized(codes, scales, spread):
    return codes.astype(F32) * jnp.dot(scales, spread, preferred_element_type=F32)


def table_kernel(codes_ref, scales_ref, table_ref):
    spread = spreader(scales_ref.shape[1])
    for start in range(0, codes_ref.shape[0], 256):
        part = pl.ds(start, 256)
        table = dequantized(codes_ref[part, :], scales_ref[part, :], spread)
        table_ref[part, :] = table.astype(BF)


def fetch_kernel(asked_ref, table_ref, out_ref):
    senders, cap = asked_ref.shape
    stride = table_ref.shape[0] // cap
    asked = asked_ref[...].astype(F32).astype(BF)
    part, width = 8 * senders, 8 * stride
    pick = (iota((part, senders), 0) // 8 == iota((part, senders), 1)).astype(F32).astype(BF)
    lists = jnp.dot(pick, asked, preferred_element_type=F32)
    entry = iota((part, 1), 0) % 8
    halves = []
    for at in range(cap // 8):
        own = iota((part, cap), 1) == iota((part, cap), 0) % 8 + at * 8
        offset = jnp.sum(jnp.where(own, lists, 0.0), axis=1, keepdims=True).astype(jnp.int32)
        target = jnp.where(offset >= 0, entry * stride + offset, -1)
        chosen = (iota((part, width), 1) == target).astype(F32).astype(BF)
        got = jnp.dot(chosen, table_ref[pl.ds(at * width, width), :], preferred_element_type=F32)
        halves.append(got.reshape(senders, 8, C))
        if at % 2 == 1:
            both = jnp.concatenate(halves, axis=1)
            out_ref[:, pl.ds((at - 1) * 8, 16), :] = both.astype(BF)
            halves = []


def sigmoid(values):
    return 0.5 + 0.5 * jnp.tanh(0.5 * values)


def train_kernel(
    place_ref,
    slots_ref,
    code_ref,
    fetched_ref,
    gain_ref,
    upstream_ref,
    *refs,
):
    weight_refs, refs = refs[: LAYERS * TAPS], refs[LAYERS * TAPS :]
    slot_grad_ref, keep_ref, send_ref, held_ref, conv_ref, unit_ref = refs[:6]
    scale_ref, grad_ref, wide_ref, weight_grad_ref = refs[6:]
    split, x, y, core = place_ref[0], place_ref[1], place_ref[2], place_ref[3]
    steps = range(0, PACKED, STEP)
    line = iota((PACKED, C), 0)
    since = jnp.where(line >= split, line - split, line)
    until = jnp.where(line >= split, PACKED - line, split - line)

    source = iota((PACKED, 1), 0)
    source = jnp.where(source >= split, source + (LEN - split), source)
    match = iota((PACKED, 2 * LEN), 1) == source
    packer = match.astype(F32).astype(BF)
    slot = jnp.where(match, slots_ref[...].astype(F32), 0.0)
    slot = jnp.sum(slot, axis=1, keepdims=True).astype(jnp.int32)
    slots = fetched_ref.shape[0]
    chosen = (iota((PACKED, slots), 1) == slot).astype(F32).astype(BF)
    first = jnp.dot(chosen, fetched_ref[...], preferred_element_type=F32)
    held_ref[0] = first.astype(BF)

    for layer in range(LAYERS):
        gap = DILATIONS[layer]
        now = held_ref[layer].astype(F32)
        taps = [held_ref[layer]]
        for tap in (1, 2):
            moved = pltpu.roll(now, tap * gap, 0)
            taps.append(jnp.where(since >= tap * gap, moved, 0.0).astype(BF))
        conv_ref[...] = jnp.dot(
            jnp.concatenate(taps, axis=1),
            jnp.concatenate([ref[...] for ref in weight_refs[layer * TAPS :][:TAPS]], axis=0),
            preferred_element_type=F32,
        )
        gain = gain_ref[pl.ds(layer, 1), :]
        for start in steps:
            part = pl.ds(start, STEP)
            value = conv_ref[part, :]
            center = value - jnp.mean(value, axis=1, keepdims=True)
            spread = jnp.mean(center * center, axis=1, keepdims=True)
            scale = lax.rsqrt(spread + 1e-5)
            unit = center * scale
            unit_ref[layer, part, :] = unit
            scale_ref[layer, part, :] = jnp.broadcast_to(scale, (STEP, 128))
            if layer + 1 < LAYERS:
                gained = unit * gain
                after = gained * sigmoid(gained)
                if layer % 2 == 1:
                    after = after + held_ref[layer - 1, part, :].astype(F32)
                held_ref[layer + 1, part, :] = after.astype(BF)

    upstream = jnp.dot(packer, upstream_ref[...], preferred_element_type=F32)
    grad_ref[...] = upstream
    held_ref[5] = upstream.astype(BF)

    gain_rows = [None] * LAYERS
    for layer in reversed(range(LAYERS)):
        gap = DILATIONS[layer]
        gain = gain_ref[pl.ds(layer, 1), :]
        total = jnp.zeros((8, C), F32)
        for start in steps:
            part = pl.ds(start, STEP)
            unit = unit_ref[layer, part, :]
            scale = scale_ref[layer, part, :]
            gained = unit * gain
            gate = sigmoid(gained)
            inner = grad_ref[part, :] * (gate * (1.0 + gained * (1.0 - gate)))
            total = total + jnp.sum((inner * unit).reshape(STEP // 8, 8, C), axis=0)
            inner = inner * gain
            mean = jnp.mean(inner, axis=1, keepdims=True)
            slope = jnp.mean(inner * unit, axis=1, keepdims=True)
            outer = inner - mean - unit * slope
            conv_ref[part, :] = outer * jnp.concatenate([scale, scale], axis=1)
        gain_rows[layer] = jnp.sum(total, axis=0, keepdims=True)
        now = conv_ref[...]
        wide_ref[:, 0:C] = now.astype(BF)
        for tap in (1, 2):
            moved = pltpu.roll(now, PACKED - tap * gap, 0)
            moved = jnp.where(until > tap * gap, moved, 0.0)
            wide_ref[:, tap * C : (tap + 1) * C] = moved.astype(BF)

        below = jnp.zeros((PACKED, C), F32)
        for tap in range(TAPS):
            kernel = weight_refs[layer * TAPS + tap][...]
            below = below + lax.dot_general(
                wide_ref[:, tap * C : (tap + 1) * C], kernel, NT, preferred_element_type=F32
            )
        if layer % 2 == 0:
            if layer == 2:
                skip = held_ref[5].astype(F32)
            else:
                skip = held_ref[4].astype(F32)
            below = below + skip
        rounded = below.astype(BF)
        grad_ref[...] = rounded.astype(F32)
        if layer == 2:
            held_ref[4] = rounded

        weight_grad = lax.dot_general(
            held_ref[layer], wide_ref[...], TN, preferred_element_type=F32
        )
        for tap in range(TAPS):
            weight_grad_ref[pl.ds(tap * C, C), :] = weight_grad[:, tap * C : (tap + 1) * C]

        for pair in range(4):
            even = weight_grad_ref[pl.ds(2 * pair * PIECE, PIECE), :]
            odd = weight_grad_ref[pl.ds((2 * pair + 1) * PIECE, PIECE), :]
            tail = jnp.zeros((TAIL, C), F32)
            even_tail = tail
            if layer == 0 and pair == 0:
                exact = jnp.concatenate(gain_rows + gain_rows, axis=0)
                high = exact.astype(BF).astype(F32)
                even_tail = jnp.where(iota((TAIL, C), 0) < LAYERS, high, exact - high)
            even = jnp.concatenate([even, even_tail], axis=0)
            odd = jnp.concatenate([odd, tail], axis=0)
            place = ((pair - y + 4) % 4) * 4 + (layer - x + 4) % 4
            keep_ref[place] = jnp.where(core == 0, even, odd).astype(BF)
            send_ref[place] = jnp.where(core == 0, odd, even).astype(BF)

    mine = grad_ref[...].astype(BF)
    for start in range(0, slots, 256):
        here = iota((256, PACKED), 0) + start == code_ref[...]
        here = here.astype(F32).astype(BF)
        summed = jnp.dot(here, mine, preferred_element_type=F32)
        slot_grad_ref[pl.ds(start, 256), :] = summed.astype(BF)


def settle(total):
    tail = total[PIECE:SLAB, :]
    exact = tail + pltpu.roll(tail, LAYERS, 0)
    high = exact.astype(BF).astype(F32)
    tail = jnp.where(iota((TAIL, C), 0) < LAYERS, high, exact - high)
    return jnp.concatenate([total[:PIECE, :], tail], axis=0).astype(BF)


def core_sum_kernel(keep_ref, got_ref, *out_refs):
    for at in range(16):
        total = keep_ref[at].astype(F32) + got_ref[at].astype(F32)
        out_refs[at // 4][at % 4] = settle(total)


def four_sum_kernel(a_ref, b_ref, c_ref, d_ref, *out_refs):
    for at in range(a_ref.shape[0]):
        left = a_ref[at].astype(F32) + b_ref[at].astype(F32)
        right = c_ref[at].astype(F32) + d_ref[at].astype(F32)
        out_refs[at][0] = settle(left + right)


def last_sum_kernel(a_ref, b_ref, *refs):
    slab = settle(a_ref[0].astype(F32) + b_ref[0].astype(F32)).astype(F32)
    rows = refs[0][0].astype(F32) + refs[1][0].astype(F32)
    refs[2][...] = jnp.concatenate([rows, slab], axis=0).astype(BF)


def part_kernel(*refs):
    for at, ref in zip((0, 1, 3, 2), refs[:4]):
        both = ref[...].astype(F32)
        refs[4][at] = both[:C].astype(BF)
        refs[5][at] = both[C:].astype(BF)


def spread_kernel(count, plan, first, place_ref, *refs):
    sources, refs = refs[:count], refs[count:]
    if not first:
        gain_before, refs = refs[1], refs[2:]
    conv_hbm, gain_ref, wide_ref, sems = refs
    x, y, core = place_ref[1], place_ref[2], place_ref[3]
    gain_ref[...] = jnp.zeros_like(gain_ref) if first else gain_before[...]
    leaving = []
    for at, (buffer, inner, along_x, along_y, other) in enumerate(plan):
        layer = (x + along_x) % 4
        side = core if other == 0 else 1 - core
        number = layer * 8 + ((y + along_y) % 4) * 2 + side
        block = sources[buffer][inner].astype(F32)
        wide_ref[at] = block[:PIECE, :]
        copy = pltpu.make_async_copy(
            wide_ref.at[at],
            conv_hbm.at[pl.ds(pl.multiple_of(number * PIECE, PIECE), PIECE)],
            sems.at[at],
        )
        copy.start()
        leaving.append(copy)

        @pl.when(number == 0)
        def _():
            tail = block[PIECE:, :]
            gain_ref[...] = (tail + pltpu.roll(tail, LAYERS, 0))[:LAYERS, :]

    for copy in leaving:
        copy.wait()


def spread(place, blocks, plan, before=None):
    outs = [shape((LAYERS * TAPS * C, C), F32), shape((LAYERS, C), F32)]
    count = len(blocks)
    args, specs, aliases = [place] + blocks, [SMEM] + [VMEM] * count, {}
    if before is not None:
        args, specs = args + list(before), specs + [HBM, VMEM]
        aliases = {count + 1: 0}
    return pl.pallas_call(
        functools.partial(spread_kernel, count, plan, before is None),
        out_shape=outs,
        in_specs=specs,
        out_specs=[HBM, VMEM],
        input_output_aliases=aliases,
        scratch_shapes=[
            pltpu.VMEM((len(plan), PIECE, C), F32),
            pltpu.SemaphoreType.DMA((len(plan),)),
        ],
        compiler_params=pltpu.CompilerParams(vmem_limit_bytes=8 * 1024 * 1024),
        cost_estimate=pl.CostEstimate(flops=0, bytes_accessed=1 << 21, transcendentals=0),
    )(*args)


def scatter_kernel(place_ref, code_ref, got_ref, keep_ref, send_ref):
    y, core = place_ref[2], place_ref[3]
    senders = got_ref.shape[0]
    lines = code_ref.shape[1]
    for pair in range(4):
        if pair % 2 == 0:
            both = got_ref[:, pl.ds(pair * 8, 16), :].astype(F32).reshape(senders, 2, 8, C)
        got = both[:, pair % 2].reshape(lines, C).astype(BF)
        here = iota((2 * C, lines), 0) + pair * 2 * C == code_ref[pl.ds(pair, 1), :]
        here = here.astype(F32).astype(BF)
        total = jnp.dot(here, got, preferred_element_type=F32)
        even, odd = total[:C], total[C:]
        apart = pair ^ y
        place = jnp.where(apart == 3, 1, jnp.where(apart == 0, 0, apart + 1))
        keep_ref[place] = jnp.where(core == 0, even, odd).astype(BF)
        send_ref[place] = jnp.where(core == 0, odd, even).astype(BF)


def row_sum_kernel(keep_ref, got_ref, *out_refs):
    half = keep_ref.shape[0] // 2
    total = (keep_ref[...].astype(F32) + got_ref[...].astype(F32)).astype(BF)
    out_refs[0][...] = total[:half]
    out_refs[1][...] = total[half:]


def adagrad_kernel(place_ref, *refs):
    own_ref, across_ref, codes_ref, scales_ref, accum_ref = refs[:5]
    rows_hbm, next_ref, rows_ref, sems = refs[5:]
    spread = spreader(scales_ref.shape[1])
    y, core = place_ref[2], place_ref[3]
    same = iota((C, C), 0) == iota((C, C), 1)
    half = C // 2
    leaving = []
    for at in range(8):
        side = core if at < 4 else 1 - core
        number = ((y + at % 4) % 4) * 2 + side
        part = pl.ds(pl.multiple_of(number * C, C), C)
        gradient = (own_ref[at] if at < 4 else across_ref[at - 4]).astype(F32)
        lines = [accum_ref[pl.ds(2 * number + side, 1), :] for side in range(2)]
        line = jnp.concatenate(lines, axis=1)
        grown = jnp.sum(jnp.where(same, line, 0.0), axis=1, keepdims=True)
        grown = grown + jnp.mean(gradient * gradient, axis=1, keepdims=True)
        table = dequantized(codes_ref[part, :], scales_ref[part, :], spread)
        rows_ref[at] = table - LEARN_RATE * gradient * lax.rsqrt(grown)
        copy = pltpu.make_async_copy(rows_ref.at[at], rows_hbm.at[part], sems.at[at])
        copy.start()
        leaving.append(copy)
        line = jnp.sum(jnp.where(same, grown, 0.0), axis=0, keepdims=True)
        next_ref[pl.ds(2 * number, 1), :] = line[:, :half]
        next_ref[pl.ds(2 * number + 1, 1), :] = line[:, half:]
    for copy in leaving:
        copy.wait()


def shifted(values, axis, size, offset):
    return lax.ppermute(values, axis, [(i, (i + offset) % size) for i in range(size)])


def crossed(values, axis, size, bits):
    return lax.ppermute(values, axis, [(i, i ^ bits) for i in range(size)])


def after(values, *others):
    return lax.optimization_barrier((values, *others))[0]


def body(lengths, slots, requests, counts, codes, scales, accum, conv_weight, norm_gain, upstream):
    table_axes = ("x", "z")
    owners = requests.shape[1]
    cap = requests.shape[2]
    rows = codes.shape[0]
    stride = rows // cap
    split = lengths[0, 0]
    place = jnp.stack(
        [split, lax.axis_index("x"), lax.axis_index("y"), lax.axis_index("core")]
    ).astype(jnp.int32)

    entry = jnp.arange(cap, dtype=jnp.int32)[None, :]
    wanted = jnp.where(entry < counts[0][:, None], requests[0] - entry * stride, -1)
    asked = lax.all_to_all(wanted, table_axes, split_axis=0, concat_axis=0, tiled=True)

    order = jnp.arange(PACKED, dtype=jnp.int32)
    order = order + jnp.where(order >= split, LEN - split, 0)
    match = order[:, None] == jnp.arange(2 * LEN, dtype=jnp.int32)[None, :]
    packed = jnp.sum(jnp.where(match, slots.reshape(1, 2 * LEN), 0), axis=1)

    table = call(table_kernel, shape((rows, C), BF), [codes, scales], flops=1 << 24)
    sending = call(
        fetch_kernel, shape((owners, cap, C), BF), [asked, table], flops=1 << 30
    )
    fetched = lax.all_to_all(
        sending, table_axes, split_axis=0, concat_axis=0, tiled=True
    ).reshape(owners * cap, C)

    target = jnp.where(asked >= 0, asked + entry * stride, -1)
    target = target.reshape(owners, 4, 8).transpose(1, 0, 2).reshape(4, 8 * owners)
    fetched, target = lax.optimization_barrier((fetched, target))

    slab16 = shape((16, SLAB, C), BF)
    slot_grad, keep, send = call(
        train_kernel,
        [shape((owners * cap, C), BF), slab16, slab16],
        [
            place,
            slots.reshape(1, 2 * LEN),
            packed.reshape(1, PACKED),
            fetched,
            norm_gain,
            upstream.reshape(2 * LEN, C),
            *[conv_weight[layer, tap] for layer in range(LAYERS) for tap in range(TAPS)],
        ],
        specs=[SMEM] + [VMEM] * 17,
        scratch=[
            pltpu.VMEM((LAYERS + 2, PACKED, C), BF),
            pltpu.VMEM((PACKED, C), F32),
            pltpu.VMEM((LAYERS, PACKED, C), F32),
            pltpu.VMEM((LAYERS, PACKED, 128), F32),
            pltpu.VMEM((PACKED, C), F32),
            pltpu.VMEM((PACKED, TAPS * C), BF),
            pltpu.VMEM((TAPS * C, C), F32),
        ],
        flops=1 << 32,
        limit=16,
    )

    got = crossed(send, "core", 2, 1)
    returned = lax.all_to_all(
        slot_grad.reshape(owners, cap, C), table_axes, split_axis=0, concat_axis=0, tiled=True
    )
    slab4, slab1 = shape((4, SLAB, C), BF), shape((1, SLAB, C), BF)
    block4 = shape((4, C, C), BF)

    parts = call(core_sum_kernel, [slab4] * 4, [keep, got])
    parts = [parts[0]] + [shifted(parts[k], "y", 4, k) for k in (2, 1, 3)]
    parts = call(four_sum_kernel, [slab1] * 4, parts)
    parts = [parts[0]] + [shifted(parts[k], "x", 4, k) for k in (2, 1, 3)]
    keep_rows, send_rows = call(
        scatter_kernel,
        [block4, block4],
        [place, target, after(returned, *parts[1:])],
        specs=[SMEM, VMEM, VMEM],
        flops=1 << 29,
    )
    sums = [keep_rows, crossed(send_rows, "core", 2, 1)]
    parts, sums = lax.optimization_barrier((parts, sums))

    (part,) = call(four_sum_kernel, [slab1], parts)
    keep_rows, send_rows = call(row_sum_kernel, [shape((2, C, C), BF)] * 2, sums)
    parts = [part] + [crossed(part, "z", 8, k) for k in (1, 2, 3)]
    sums = [keep_rows, crossed(send_rows, "y", 4, 1)]
    parts, sums = lax.optimization_barrier((parts, sums))
    (part,) = call(four_sum_kernel, [slab1], parts)
    keep_rows, send_rows = call(row_sum_kernel, [shape((1, C, C), BF)] * 2, sums)
    parts = [part, crossed(part, "z", 8, 6)]
    sums = [keep_rows, crossed(send_rows, "y", 4, 3)]
    parts, sums = lax.optimization_barrier((parts, sums))

    part = call(last_sum_kernel, shape((C + SLAB, C), BF), parts + sums)
    parts = [part] + [shifted(part, "y", 4, -k) for k in (1, 3, 2)]
    mine, parts = call(part_kernel, [block4, slab4], parts)
    later = [shifted(parts, "x", 4, -k) for k in (1, 3, 2)]
    across = crossed(mine, "core", 2, 1)
    new_rows, next_accum = call(
        adagrad_kernel,
        [shape((rows, C), F32), shape((rows // 128, 128), F32)],
        [place, mine, across, codes, scales, accum.reshape(rows // 128, 128)],
        specs=[SMEM] + [VMEM] * 5,
        out_specs=[HBM, VMEM],
        scratch=[pltpu.VMEM((8, C, C), F32), pltpu.SemaphoreType.DMA((8,))],
    )
    plan = [(at, inner, 0, inner, at) for at in range(2) for inner in range(4)]
    filled = spread(place, [parts, crossed(parts, "core", 2, 1)], plan)
    later = after(later, next_accum, filled)
    order = (1, 3, 2)
    plan = [(at, inner, order[at], inner, 0) for at in range(3) for inner in range(4)]
    beyond = [crossed(part, "core", 2, 1) for part in later]
    filled = spread(place, later, plan, filled)
    plan = [(at, inner, order[at], inner, 1) for at in range(3) for inner in range(4)]
    grad_conv, grad_gain = spread(place, beyond, plan, filled)
    return (
        new_rows,
        next_accum.reshape(rows),
        grad_conv.reshape(conv_weight.shape),
        grad_gain,
    )


def solution(mesh):
    fine = Mesh(mesh.devices.reshape(4, 8, 4, 2), ("x", "z", "y", "core"))
    every = ("x", "z", "y", "core")
    table = ("x", "z")
    return jax.shard_map(
        body,
        mesh=fine,
        in_specs=(
            P(every, None),
            P(every, None),
            P(every, None, None),
            P(every, None),
            P(table, None),
            P(table, None),
            P(table),
            P(),
            P(),
            P(every, None, None),
        ),
        out_specs=(P(table, None), P(table), P(), P()),
        check_vma=False,
    )
```
